512 devices in a mesh: section: 16 (over x, z_hi), seq: 32 (over z_lo, y, core).
Axes of the slice: x: 4, y: 4, z: 16 (z_hi: 4, z_lo: 4; z = z_hi * 4 + z_lo), core: 2. Of those that a mesh axis runs over, the one named last changes fastest.
Arguments:
- queries: bfloat16 [16, 768, 4096], P('section', 'seq'), as said below
- keys: bfloat16 [16, 768, 4096], P('section', 'seq'), as said below
- values: bfloat16 [16, 768, 4096], P('section', 'seq'), may hold values from -6 to 6
- latent: bfloat16 [16, 768, 4096], P('section', 'seq'), may hold values from -6 to 6
- entering: bfloat16 [768, 4096], P('seq'), may hold values from -6 to 6
- noise_level: int32 [16], P('section'), may hold values from 0 to 15
- token_counts: int32 [16], replicated, may hold values from 384 to 768, as said below
- block_mask: int32 [16, 16], replicated, may hold values from 0 to 1, as said below
- gate_table: float32 [16, 4096], replicated, may hold values from 0.3 to 3
Outputs:
- updated: bfloat16 [16, 768, 4096], P('section', 'seq')
- advanced: bfloat16 [16, 768, 4096], P('section', 'seq')
The draws below stay inside these ranges and needn't reach their ends.
Inputs may be any that keep to these rules, and one draw needn't show every extreme that they name: `queries`: entries lie in -6 to 6. `keys`: entries lie in -4 to 4. `token_counts`: at least 384 tokens of every block are valid; one block is full in every draw. block_mask[s, s] = 1 and block_mask[s, t] = 0 for t > s; blocks before s may be 0 or 1.
All inputs are finite; a program needn't handle non-finite values.
Results may differ from the reference program's by a relative error of at most 0.0065.
Values may be sent and summed in bfloat16 or wider, within the bound.
No kernel may reach another device: no remote copies, remote signals or barrier semaphores. Data moves between devices by JAX's collectives and lax.ppermute only.
A program may use at most 64 MiB of HBM per device.

```python
import math
import jax
import jax.numpy as jnp
from jax import lax

HEADS = 32
HD = 128
LEVELS = 16
SECTIONS = 16
BLOCK_TOK = 768
F = 4096


def aligned_signs(key):
    flips = jax.random.bernoulli(jax.random.fold_in(key, 77), 0.5, (HD,))
    return jnp.where(flips, 1.0, -1.0).astype(jnp.float32)


def draw_queries(key, part):
    key = jax.random.fold_in(key, 1)
    sample = jnp.clip(3.0 * jax.random.normal(key, (SECTIONS, BLOCK_TOK, F), jnp.float32), -6.0, 6.0)
    return sample.astype(jnp.bfloat16)


def draw_keys(key, part):
    signs = aligned_signs(key)
    key = jax.random.fold_in(key, 2)
    lanes = jnp.arange(HD)
    first = 4.0 * signs
    second = jnp.where(lanes < 1, 0.0, 4.0 * signs)
    third = jnp.where(lanes < 2, 0.0, 4.0 * signs)
    planted = jnp.stack([first, second, third], axis=0)
    sample = jnp.clip(jax.random.normal(key, (SECTIONS, BLOCK_TOK, F), jnp.float32), -4.0, 4.0)
    sample = sample.at[0, 3:6, 0:HD].set(planted)
    return sample.astype(jnp.bfloat16)


def draw_token_counts(key, part):
    key = jax.random.fold_in(key, 3)
    counts = jax.random.randint(jax.random.fold_in(key, 1), (SECTIONS,), BLOCK_TOK // 2, BLOCK_TOK + 1)
    full_one = jax.random.randint(jax.random.fold_in(key, 2), (), 0, SECTIONS)
    counts = jnp.where(jnp.arange(SECTIONS) == full_one, BLOCK_TOK, counts)
    return counts.astype(jnp.int32)


def draw_block_mask(key, part):
    key = jax.random.fold_in(key, 4)
    coins = jax.random.randint(key, (SECTIONS, SECTIONS), 0, 4)
    rows = jnp.arange(SECTIONS)[:, None]
    cols = jnp.arange(SECTIONS)[None, :]
    earlier = jnp.where(coins > 0, 1, 0)
    result = jnp.where(cols < rows, earlier, jnp.where(cols == rows, 1, 0))
    return result.astype(jnp.int32)


def set_ends(entries, key, smallest, largest):
    spot = [jax.random.randint(jax.random.fold_in(key, axis), (), 0, length) for axis, length in enumerate(entries.shape)]
    main_axis = entries.shape.index(max(entries.shape))
    next_to = spot[:main_axis] + [(spot[main_axis] + 1) % entries.shape[main_axis]] + spot[main_axis + 1:]
    return entries.at[tuple(spot)].set(smallest).at[tuple(next_to)].set(largest)


def block_levels(rng, extent, split, smallest, largest):
    factor_of, own = 1.0, jax.random.fold_in(rng, 6)
    for dim, blocks in split:
        steps = jnp.exp(jax.random.uniform(jax.random.fold_in(own, dim), (blocks,), jnp.float32, smallest / len(split), largest / len(split)))
        factor_of = factor_of * jnp.repeat(steps, extent[dim] // blocks).reshape([-1 if axis == dim else 1 for axis in range(len(extent))])
    return factor_of


def scatter_about(stream_key, shape, scale, most, shards=(), kind=jnp.bfloat16):
    gain = block_levels(stream_key, shape, shards, -0.22, 0.18) if shards else 1.0
    values = jax.random.normal(stream_key, shape, jnp.float32) * scale * gain
    return jnp.minimum(jnp.maximum(values, -most), most).astype(kind)


def setup_inputs(seed: int = 0) -> dict:
    splits = jax.random.split(jax.random.key(seed), 10)
    return {
        "queries": draw_queries(jax.random.fold_in(splits[9], 71), 0),
        "keys": draw_keys(jax.random.fold_in(splits[9], 71), 0),
        "values": scatter_about(splits[2], (SECTIONS, BLOCK_TOK, F), 1.0, 6.0, ((0, 16), (1, 32))),
        "latent": scatter_about(splits[3], (SECTIONS, BLOCK_TOK, F), 1.0, 6.0, ((0, 16), (1, 32))),
        "entering": scatter_about(splits[4], (BLOCK_TOK, F), 1.0, 6.0, ((0, 32),)),
        "noise_level": set_ends(jax.random.randint(splits[5], (SECTIONS,), 0, LEVELS), jax.random.fold_in(splits[5], 1), 0, LEVELS - 1).astype(jnp.int32),
        "token_counts": draw_token_counts(jax.random.fold_in(splits[9], 71), 0),
        "block_mask": draw_block_mask(jax.random.fold_in(splits[9], 71), 0),
        "gate_table": jnp.clip(jnp.exp(jax.random.uniform(splits[8], (LEVELS, F), jnp.float32, math.log(0.3), math.log(3.0))), 0.3, 3.0),
    }


def reference(queries, keys, values, latent, entering, noise_level, token_counts, block_mask, gate_table):
    positions = jnp.arange(BLOCK_TOK, dtype=jnp.int32)
    allowed = (block_mask[:, :, None] == 1) & (positions[None, None, :] < token_counts[None, :, None])
    key_heads = keys.reshape(SECTIONS * BLOCK_TOK, HEADS, HD)
    value_heads = values.reshape(SECTIONS * BLOCK_TOK, HEADS, HD)
    scale = 1.0 / jnp.sqrt(jnp.float32(HD))

    def one_section(section_id):
        query_rows = lax.dynamic_index_in_dim(queries, section_id, 0, keepdims=False).reshape(BLOCK_TOK, HEADS, HD)
        usable = lax.dynamic_index_in_dim(allowed, section_id, 0, keepdims=False).reshape(SECTIONS * BLOCK_TOK)

        def one_head(head_id):
            query_head = lax.dynamic_index_in_dim(query_rows, head_id, 1, keepdims=False)
            key_head = lax.dynamic_index_in_dim(key_heads, head_id, 1, keepdims=False)
            value_head = lax.dynamic_index_in_dim(value_heads, head_id, 1, keepdims=False)
            scores = jnp.dot(query_head, key_head.T, preferred_element_type=jnp.float32) * scale
            scores = jnp.where(usable[None, :], scores, jnp.float32(-1e+30))
            peak = lax.optimization_barrier(jnp.max(scores, axis=1, keepdims=True))
            weights = jnp.where(usable[None, :], jnp.exp(scores - peak), jnp.float32(0.0))
            denominator = lax.optimization_barrier(jnp.sum(weights, axis=1, keepdims=True))
            numerator = jnp.dot(weights.astype(jnp.bfloat16), value_head, preferred_element_type=jnp.float32)
            return (numerator / denominator).astype(jnp.bfloat16)
        per_head = lax.map(one_head, jnp.arange(HEADS, dtype=jnp.int32))
        return jnp.transpose(per_head, (1, 0, 2))
    attended = lax.map(one_section, jnp.arange(SECTIONS, dtype=jnp.int32))
    wide = attended.astype(jnp.float32).reshape(SECTIONS, BLOCK_TOK, F)
    normed = wide / jnp.sqrt(lax.optimization_barrier(jnp.mean(wide * wide, axis=-1, keepdims=True)) + 1e-06)
    gates = gate_table[noise_level]
    updated = (latent.astype(jnp.float32) + gates[:, None, :] * normed).astype(jnp.bfloat16)
    advanced = jnp.concatenate([entering[None], updated[:-1]], axis=0)
    return (updated, advanced)
```

```python
import math

import jax
import jax.numpy as jnp
from jax import lax
from jax.experimental import pallas as pl
from jax.experimental.pallas import tpu as pltpu
from jax.sharding import Mesh
from jax.sharding import PartitionSpec as P

HD = 128
HEADS = 32
ROWS = 24
QUARTER = 192
BLOCK = 768
STAT = 16
SCALE = math.log2(math.e) / math.sqrt(HD)
LOW = -1e30
f32 = jnp.float32
bf16 = jnp.bfloat16

VM = pl.BlockSpec(memory_space=pltpu.VMEM)
SM = pl.BlockSpec(memory_space=pltpu.SMEM)
PARAMS = pltpu.CompilerParams(vmem_limit_bytes=48 * 2**20)
HEAD_AXES = ("zh", "zl", "c")


def pack_kernel(q_ref, k_ref, v_ref, o_ref):
    for i, ref in enumerate((q_ref, k_ref, v_ref)):
        for h in range(HEADS):
            o_ref[h, i] = ref[0, :, h * HD : (h + 1) * HD]


def pack(queries, keys, values):
    return pl.pallas_call(
        pack_kernel,
        out_shape=jax.ShapeDtypeStruct((HEADS, 3, ROWS, HD), bf16),
        in_specs=[VM] * 3,
        out_specs=VM,
        compiler_params=PARAMS,
    )(queries, keys, values)


def token_of(shape, dim, y):
    i = lax.broadcasted_iota(jnp.int32, shape, dim)
    one, nil = jnp.int32(1), jnp.int32(0)
    part = sum(jnp.where(i >= e * QUARTER, one, nil) for e in (1, 2, 3))
    inner = i - part * QUARTER
    run = sum(jnp.where(inner >= e * 48, one, nil) for e in (1, 2, 3))
    return inner + run * (QUARTER - 48) + ((y + part) & 3) * 48


def attend_kernel(
    count_ref, flag_ref, y_ref, q0, q1, q2, q3, kv0, kv1, kv2, kv3, o_ref,
    q_sc, k_sc, v_sc, m_sc, acc_sc, s0, s1, p0, p1, a0, a1, units,
):
    def build(e, n):
        slot, t = e // 4, e % 4
        active = flag_ref[slot * 4, t]
        for g in range(1, 4):
            active = active | flag_ref[slot * 4 + g, t]

        @pl.when(active == 1)
        def _():
            units[0, n] = slot
            units[1, n] = t

        return n + active

    for i in range(2):
        units[0, i] = 4
        units[1, i] = 0
    n = lax.fori_loop(0, 16, build, jnp.int32(2))
    for i in range(4):
        units[0, n + i] = 4
        units[1, n + i] = 0

    for slot, ref in enumerate((q0, q1, q2, q3)):
        q_sc[slot] = ref[...].reshape(BLOCK, HD)

    token = token_of((BLOCK, HD), 0, y_ref[0])
    token_row = token_of((STAT, BLOCK), 1, y_ref[0])
    for t in range(4):
        k = jnp.concatenate([ref[t, :, 0].reshape(QUARTER, HD) for ref in (kv0, kv1, kv2, kv3)])
        v = jnp.concatenate([ref[t, :, 1].reshape(QUARTER, HD) for ref in (kv0, kv1, kv2, kv3)])
        valid = token < count_ref[t]
        k_sc[t] = jnp.where(valid, k, jnp.broadcast_to(k[0:1], k.shape))
        v_sc[t, :HD] = jnp.where(valid, v, jnp.zeros_like(v)).T
        v_sc[t, HD:] = jnp.where(token_row < count_ref[t], 1.0, 0.0).astype(bf16)

    m_sc[...] = jnp.full(m_sc.shape, LOW, f32)
    acc_sc[...] = jnp.zeros(acc_sc.shape, f32)
    lane = lax.broadcasted_iota(jnp.int32, (8, BLOCK), 1)

    def score(i, s):
        slot = jnp.minimum(units[0, i], 3)
        s[...] = lax.dot_general(
            k_sc[units[1, i]], q_sc[slot], (((1,), (1,)), ((), ())), preferred_element_type=f32
        )

    def weigh(i, s, p, a):
        slot, t = units[0, i], units[1, i]
        first = jnp.minimum(slot, 3) * 4
        flag = jnp.full((8, BLOCK), flag_ref[first, t], jnp.int32)
        for g in range(1, 4):
            flag = jnp.where(lane >= g * QUARTER, flag_ref[first + g, t], flag)
        on = flag == 1
        old = m_sc[slot]
        top = jnp.max(s[...], axis=0, keepdims=True) * SCALE
        new = jnp.where(on, jnp.maximum(old, top), old)
        m_sc[slot] = new
        a[...] = jnp.exp2(old - new)
        p[...] = jnp.exp2(s[...] * SCALE - jnp.where(on, new, -LOW)[:1]).astype(bf16)

    def gather(i, p, a):
        slot = units[0, i]
        part = jnp.dot(v_sc[units[1, i]], p[...], preferred_element_type=f32)
        acc_sc[slot] = acc_sc[slot] * a[:1] + part

    def step(h, carry):
        i = 2 + 2 * h
        gather(i - 2, p0, a0)
        weigh(i - 1, s1, p1, a1)
        score(i, s0)
        gather(i - 1, p1, a1)
        weigh(i, s0, p0, a0)
        score(i + 1, s1)
        return carry

    p0[...] = jnp.zeros(p0.shape, bf16)
    p1[...] = jnp.zeros(p1.shape, bf16)
    s1[...] = jnp.zeros(s1.shape, f32)
    lax.fori_loop(0, (n + 1) // 2, step, 0)

    for slot in range(4):
        total = acc_sc[slot, HD : HD + 1]
        some = total > 0.0
        safe = jnp.where(some, total, 1.0)
        o_ref[slot, :HD] = (acc_sc[slot, :HD] * (1.0 / safe)).astype(bf16)
        level = jnp.where(some, m_sc[slot, :1] + jnp.log2(safe), LOW)
        hi = level.astype(bf16)
        mid = (level - hi.astype(f32)).astype(bf16)
        lo = (level - hi.astype(f32) - mid.astype(f32)).astype(bf16)
        pad = jnp.zeros((STAT - 3, BLOCK), bf16)
        o_ref[slot, HD:] = jnp.concatenate([hi, mid, lo, pad], axis=0)


def attend(counts, flags, y, qs, kvs):
    vmem = pltpu.VMEM
    return pl.pallas_call(
        attend_kernel,
        out_shape=jax.ShapeDtypeStruct((4, HD + STAT, BLOCK), bf16),
        in_specs=[SM] * 3 + [VM] * 8,
        out_specs=VM,
        scratch_shapes=[
            vmem((4, BLOCK, HD), bf16),
            vmem((4, BLOCK, HD), bf16),
            vmem((4, HD + STAT, BLOCK), bf16),
            vmem((5, 8, BLOCK), f32),
            vmem((5, HD + STAT, BLOCK), f32),
            vmem((BLOCK, BLOCK), f32),
            vmem((BLOCK, BLOCK), f32),
            vmem((BLOCK, BLOCK), bf16),
            vmem((BLOCK, BLOCK), bf16),
            vmem((8, BLOCK), f32),
            vmem((8, BLOCK), f32),
            pltpu.SMEM((2, 24), jnp.int32),
        ],
        compiler_params=PARAMS,
    )(counts, flags, y, *qs, *kvs)


def merge_kernel(x_ref, r0, r1, r2, r3, o_ref):
    refs = (r0, r1, r2, r3)
    levels = []
    for k, ref in enumerate(refs):
        stat = ref[HD:].astype(f32)
        level = stat[0:1] + stat[1:2] + stat[2:3]
        levels.append(jnp.where(x_ref[0] >= k, level, LOW) if k else level)
    top = jnp.maximum(jnp.maximum(levels[0], levels[1]), jnp.maximum(levels[2], levels[3]))
    shares = [jnp.exp2(level - top) for level in levels]
    whole = shares[0] + shares[1] + shares[2] + shares[3]
    total = sum(ref[:HD].astype(f32) * (share / whole) for ref, share in zip(refs, shares))
    o_ref[...] = total.T.astype(bf16).reshape(HEADS, ROWS, HD)


def merge(x, parts):
    return pl.pallas_call(
        merge_kernel,
        out_shape=jax.ShapeDtypeStruct((HEADS, ROWS, HD), bf16),
        in_specs=[SM] + [VM] * 4,
        out_specs=VM,
        compiler_params=PARAMS,
    )(x, *parts)


def finish_kernel(level_ref, r_ref, latent_ref, gate_ref, o_ref):
    squares = jnp.zeros((ROWS, HD), f32)
    for h in range(HEADS):
        wide = r_ref[h].astype(f32)
        squares = squares + wide * wide
    mean = jnp.sum(squares, axis=-1, keepdims=True) * (1.0 / (HEADS * HD))
    factor = 1.0 / jnp.sqrt(mean + 1e-06)
    mine = lax.broadcasted_iota(jnp.int32, (gate_ref.shape[0], HD), 0) == level_ref[0]
    for h in range(HEADS):
        span = slice(h * HD, (h + 1) * HD)
        gate = jnp.sum(jnp.where(mine, gate_ref[:, span], 0.0), axis=0, keepdims=True)
        wide = r_ref[h].astype(f32)
        o_ref[0, :, span] = (
            latent_ref[0, :, span].astype(f32) + gate * (wide * factor)
        ).astype(bf16)


def finish(noise_level, returned, latent, gate_table):
    return pl.pallas_call(
        finish_kernel,
        out_shape=jax.ShapeDtypeStruct(latent.shape, bf16),
        in_specs=[SM] + [VM] * 3,
        out_specs=VM,
        compiler_params=PARAMS,
    )(noise_level, returned, latent, gate_table)


def local(
    queries, keys, values, latent, entering, noise_level, token_counts, block_mask, gate_table
):
    x = lax.axis_index("x")
    y = lax.axis_index("y")
    packed = pack(queries, keys, values)
    packed = lax.all_to_all(packed, HEAD_AXES, split_axis=0, concat_axis=0, tiled=True)
    kv = packed[:, 1:3].reshape(4, 8, 2, ROWS, HD)
    q = packed[:, 0]
    kvs = [kv] + [
        lax.ppermute(kv, "y", [(source, (source - k) % 4) for source in range(4)])
        for k in (1, 2, 3)
    ]
    qs = [q] + [
        lax.ppermute(q, "x", [(source, source - k) for source in range(k, 4)]) for k in (1, 2, 3)
    ]
    padded = jnp.concatenate([block_mask, jnp.zeros_like(block_mask)], axis=0)
    flags = lax.dynamic_slice(padded, (4 * x, 4 * x), (16, 4))
    counts = lax.dynamic_slice(token_counts, (4 * x,), (4,))
    parts = attend(counts, flags, y.reshape(1), qs, kvs)
    received = [parts[0]] + [
        lax.ppermute(parts[k], "x", [(source, source + k) for source in range(4 - k)])
        for k in (1, 2, 3)
    ]
    attended = merge(x.reshape(1), received)
    returned = lax.all_to_all(attended, HEAD_AXES, split_axis=0, concat_axis=0, tiled=True)
    updated = finish(noise_level, returned, latent, gate_table)
    moved = lax.ppermute(updated, ("x", "zh"), [(s, s + 1) for s in range(15)])
    first = (x == 0) & (lax.axis_index("zh") == 0)
    advanced = jnp.where(first, entering[None], moved)
    return (updated, advanced)


def solution(mesh):
    fine = Mesh(mesh.devices.reshape(4, 4, 4, 4, 2), ("x", "zh", "zl", "y", "c"))
    section, seq = ("x", "zh"), ("zl", "y", "c")
    placed = (
        P(section, seq, None),
        P(section, seq, None),
        P(section, seq, None),
        P(section, seq, None),
        P(seq, None),
        P(section),
        P(),
        P(),
        P(),
    )
    return jax.shard_map(
        local,
        mesh=fine,
        in_specs=placed,
        out_specs=(P(section, seq, None), P(section, seq, None)),
        check_vma=False,
    )
```

```python
import math

import jax
import jax.numpy as jnp
from jax import lax
from jax.experimental import pallas as pl
from jax.experimental.pallas import tpu as pltpu
from jax.sharding import Mesh
from jax.sharding import PartitionSpec as P

HD = 128
HEADS = 32
ROWS = 24
QUARTER = 192
BLOCK = 768
STAT = 16
SCALE = math.log2(math.e) / math.sqrt(HD)
LOW = -1e30
f32 = jnp.float32
bf16 = jnp.bfloat16

VM = pl.BlockSpec(memory_space=pltpu.VMEM)
SM = pl.BlockSpec(memory_space=pltpu.SMEM)
PARAMS = pltpu.CompilerParams(vmem_limit_bytes=48 * 2**20)
HEAD_AXES = ("zh", "zl", "c")


def pack_kernel(level_ref, q_hbm, k_hbm, v_hbm, latent_hbm, o_ref, latent_ref, buf, sems):
    sources = (q_hbm, k_hbm, v_hbm, latent_hbm)
    copies = [pltpu.make_async_copy(ref, buf.at[i], sems.at[i]) for i, ref in enumerate(sources)]
    for copy in copies:
        copy.start()
    latent_ref[0, :, HEADS * HD :] = jnp.full((ROWS, HD), level_ref[0], jnp.int32).astype(
        f32
    ).astype(bf16)
    for i in range(3):
        copies[i].wait()
        for h in range(HEADS):
            o_ref[h, i] = buf[i, 0, :, h * HD : (h + 1) * HD]
    copies[3].wait()
    latent_ref[0, :, : HEADS * HD] = buf[3, 0]


def pack(level, queries, keys, values, latent):
    hbm = pl.BlockSpec(memory_space=pltpu.HBM)
    return pl.pallas_call(
        pack_kernel,
        out_shape=[
            jax.ShapeDtypeStruct((HEADS, 3, ROWS, HD), bf16),
            jax.ShapeDtypeStruct((1, ROWS, HEADS * HD + HD), bf16),
        ],
        in_specs=[SM] + [hbm] * 4,
        out_specs=[VM] * 2,
        scratch_shapes=[
            pltpu.VMEM((4, 1, ROWS, HEADS * HD), bf16),
            pltpu.SemaphoreType.DMA((4,)),
        ],
        compiler_params=PARAMS,
    )(level, queries, keys, values, latent)


def token_of(shape, dim):
    i = lax.broadcasted_iota(jnp.int32, shape, dim)
    one, nil = jnp.int32(1), jnp.int32(0)
    part = sum(jnp.where(i >= e * QUARTER, one, nil) for e in (1, 2, 3))
    inner = i - part * QUARTER
    run = sum(jnp.where(inner >= e * 48, one, nil) for e in (1, 2, 3))
    return inner + run * (QUARTER - 48) + part * 48


def attend_kernel(
    count_ref, flag_ref, place_ref, kv_ref, q_ref, o0, o1, o2, o3,
    q_sc, k_sc, v_sc, m_sc, acc_sc, s0, s1, p0, p1, a0, a1, units,
):
    def build(e, n):
        slot, t = e // 4, e % 4
        active = flag_ref[slot * 4, t]
        for g in range(1, 4):
            active = active | flag_ref[slot * 4 + g, t]

        @pl.when(active == 1)
        def _():
            units[0, n] = slot
            units[1, n] = t

        return n + active

    for i in range(2):
        units[0, i] = 4
        units[1, i] = 0
    n = lax.fori_loop(0, 16, build, jnp.int32(2))
    for i in range(4):
        units[0, n + i] = 4
        units[1, n + i] = 0

    for slot in range(4):
        q_sc[slot] = q_ref[jnp.minimum(place_ref[0] + slot, 3)].reshape(BLOCK, HD)

    token = token_of((BLOCK, HD), 0)
    token_row = token_of((STAT, BLOCK), 1)
    for t in range(4):
        k = jnp.concatenate([kv_ref[y, t, :, 0].reshape(QUARTER, HD) for y in range(4)])
        v = jnp.concatenate([kv_ref[y, t, :, 1].reshape(QUARTER, HD) for y in range(4)])
        valid = token < count_ref[t]
        k_sc[t] = jnp.where(valid, k, jnp.broadcast_to(k[0:1], k.shape))
        v_sc[t, :HD] = jnp.where(valid, v, jnp.zeros_like(v)).T
        v_sc[t, HD:] = jnp.where(token_row < count_ref[t], 1.0, 0.0).astype(bf16)

    m_sc[...] = jnp.full(m_sc.shape, LOW, f32)
    acc_sc[...] = jnp.zeros(acc_sc.shape, f32)
    lane = lax.broadcasted_iota(jnp.int32, (8, BLOCK), 1)

    def score(i, s):
        slot = jnp.minimum(units[0, i], 3)
        s[...] = lax.dot_general(
            k_sc[units[1, i]], q_sc[slot], (((1,), (1,)), ((), ())), preferred_element_type=f32
        )

    def weigh(i, s, p, a):
        slot, t = units[0, i], units[1, i]
        first = jnp.minimum(slot, 3) * 4
        flag = jnp.full((8, BLOCK), flag_ref[first, t], jnp.int32)
        for g in range(1, 4):
            flag = jnp.where(lane >= g * QUARTER, flag_ref[first + g, t], flag)
        on = flag == 1
        old = m_sc[slot]
        top = jnp.max(s[...], axis=0, keepdims=True) * SCALE
        new = jnp.where(on, jnp.maximum(old, top), old)
        m_sc[slot] = new
        a[...] = jnp.exp2(old - new)
        p[...] = jnp.exp2(s[...] * SCALE - jnp.where(on, new, -LOW)[:1]).astype(bf16)

    def gather(i, p, a):
        slot = units[0, i]
        part = jnp.dot(v_sc[units[1, i]], p[...], preferred_element_type=f32)
        acc_sc[slot] = acc_sc[slot] * a[:1] + part

    def step(h, carry):
        i = 2 + 2 * h
        gather(i - 2, p0, a0)
        weigh(i - 1, s1, p1, a1)
        score(i, s0)
        gather(i - 1, p1, a1)
        weigh(i, s0, p0, a0)
        score(i + 1, s1)
        return carry

    lax.fori_loop(0, (n + 1) // 2, step, 0)

    outs = (o0, o1, o2, o3)
    for slot in range(4):
        total = acc_sc[slot, HD : HD + 1]
        some = total > 0.0
        safe = jnp.where(some, total, 1.0)
        head = (acc_sc[slot, :HD] * (1.0 / safe)).astype(bf16)
        level = jnp.where(some, m_sc[slot, :1] + jnp.log2(safe), LOW)
        hi = level.astype(bf16)
        mid = (level - hi.astype(f32)).astype(bf16)
        lo = (level - hi.astype(f32) - mid.astype(f32)).astype(bf16)
        stat = jnp.concatenate([hi, mid, lo, jnp.zeros((STAT - 3, BLOCK), bf16)], axis=0)
        outs[slot][:HD, :BLOCK] = head
        outs[slot][HD:, :BLOCK] = stat
        if slot < 3:
            outs[slot + 1][:HD, BLOCK:] = head[:, BLOCK - QUARTER :]
            outs[slot + 1][HD:, BLOCK:] = stat[:, BLOCK - QUARTER :]


def attend(counts, flags, place, q, kv):
    vmem = pltpu.VMEM
    return pl.pallas_call(
        attend_kernel,
        out_shape=[
            jax.ShapeDtypeStruct((HD + STAT, BLOCK + (QUARTER if slot else 0)), bf16)
            for slot in range(4)
        ],
        in_specs=[SM] * 3 + [VM] * 2,
        out_specs=[VM] * 4,
        scratch_shapes=[
            vmem((4, BLOCK, HD), bf16),
            vmem((4, BLOCK, HD), bf16),
            vmem((4, HD + STAT, BLOCK), bf16),
            vmem((5, 8, BLOCK), f32),
            vmem((5, HD + STAT, BLOCK), f32),
            vmem((BLOCK, BLOCK), f32),
            vmem((BLOCK, BLOCK), f32),
            vmem((BLOCK, BLOCK), bf16),
            vmem((BLOCK, BLOCK), bf16),
            vmem((8, BLOCK), f32),
            vmem((8, BLOCK), f32),
            pltpu.SMEM((2, 24), jnp.int32),
        ],
        compiler_params=PARAMS,
        cost_estimate=pl.CostEstimate(
            flops=64 * BLOCK * BLOCK * HD, bytes_accessed=8 << 20, transcendentals=16 * BLOCK * BLOCK
        ),
    )(counts, flags, place, kv, q)


def blend(stats, heads):
    levels = [stat[0:1] + stat[1:2] + stat[2:3] for stat in stats]
    top = levels[0]
    for level in levels[1:]:
        top = jnp.maximum(top, level)
    shares = [jnp.exp2(level - top) for level in levels]
    whole = sum(shares[1:], shares[0])
    total = sum(head.astype(f32) * (share / whole) for head, share in zip(heads, shares))
    return total.T.astype(bf16)


def merge_kernel(x_ref, r0, r1, r2, r3, o_ref):
    stats, heads = [r0[HD:].astype(f32)], [r0[:HD]]
    for k, ref in ((1, r1), (2, r2), (3, r3)):
        stat = ref[HD:].astype(f32)
        row = lax.broadcasted_iota(jnp.int32, stat.shape, 0)
        stats.append(jnp.where(x_ref[0] >= k, stat, jnp.where(row == 0, LOW, 0.0)))
        heads.append(ref[:HD])
    own = blend([stat[:, :BLOCK] for stat in stats], [head[:, :BLOCK] for head in heads])
    tail = blend([stat[:, BLOCK:] for stat in stats[1:]], [head[:, BLOCK:] for head in heads[1:]])
    own = own.reshape(HEADS, ROWS, HD)
    o_ref[:, 0] = own
    o_ref[:8, 1] = tail.reshape(8, ROWS, HD)
    o_ref[8:, 1] = own[: HEADS - 8]


def merge(x, parts):
    return pl.pallas_call(
        merge_kernel,
        out_shape=jax.ShapeDtypeStruct((HEADS, 2, ROWS, HD), bf16),
        in_specs=[SM] + [VM] * 4,
        out_specs=VM,
        compiler_params=PARAMS,
    )(x, *parts)


def finish_kernel(
    level_ref, first_ref, r_ref, latent_ref, latent_before_ref, entering_ref, gate_ref,
    updated_ref, advanced_ref,
):
    def update(which, level, residual):
        squares = jnp.zeros((ROWS, HD), f32)
        for h in range(HEADS):
            wide = r_ref[h, which].astype(f32)
            squares = squares + wide * wide
        mean = jnp.sum(squares, axis=-1, keepdims=True) * (1.0 / (HEADS * HD))
        factor = 1.0 / jnp.sqrt(mean + 1e-06)
        index = lax.broadcasted_iota(jnp.int32, (gate_ref.shape[0], HD), 0)
        mine = index.astype(f32) == level
        for h in range(HEADS):
            span = slice(h * HD, (h + 1) * HD)
            gate = jnp.sum(jnp.where(mine, gate_ref[:, span], 0.0), axis=0, keepdims=True)
            wide = r_ref[h, which].astype(f32)
            yield span, residual[0, :, span].astype(f32) + gate * (wide * factor)

    for span, value in update(0, level_ref[0].astype(f32), latent_ref):
        updated_ref[0, :, span] = value.astype(bf16)
    first = first_ref[0] == 1
    before = latent_before_ref[0, :1, HEADS * HD :].astype(f32)
    for span, value in update(1, before, latent_before_ref):
        advanced_ref[0, :, span] = jnp.where(first, entering_ref[:, span], value.astype(bf16))


def finish(level, first, returned, latent, latent_before, entering, gate_table):
    return pl.pallas_call(
        finish_kernel,
        out_shape=[jax.ShapeDtypeStruct(latent.shape, bf16)] * 2,
        in_specs=[SM] * 2 + [VM] * 5,
        out_specs=[VM] * 2,
        compiler_params=PARAMS,
    )(level, first, returned, latent, latent_before, entering, gate_table)


def local(
    queries, keys, values, latent, entering, noise_level, token_counts, block_mask, gate_table
):
    x = lax.axis_index("x")
    packed, latent_level = pack(noise_level, queries, keys, values, latent)
    packed = lax.all_to_all(packed, HEAD_AXES, split_axis=0, concat_axis=0, tiled=True)
    packed, latent_level = lax.optimization_barrier((packed, latent_level))
    kv = packed[:, 1:3].reshape(4, 8, 2, ROWS, HD)
    kv, packed = lax.optimization_barrier((kv, packed))
    q = lax.all_gather(packed[:, 0], "x", axis=0, tiled=False)
    kv = jnp.broadcast_to(kv[None], (4, *kv.shape))
    kv = lax.all_to_all(kv, "y", split_axis=0, concat_axis=0, tiled=True)
    onward = [(s, s + 1) for s in range(15)]
    latent_before = lax.ppermute(latent_level, ("x", "zh"), onward)
    padded = jnp.concatenate([block_mask, jnp.zeros_like(block_mask)], axis=0)
    flags = lax.dynamic_slice(padded, (4 * x, 4 * x), (16, 4))
    counts = lax.dynamic_slice(token_counts, (4 * x,), (4,))
    parts = attend(counts, flags, x.reshape(1), q, kv)
    parts, latent_before = lax.optimization_barrier((parts, latent_before))
    received = [parts[0]] + [
        lax.ppermute(parts[k], "x", [(source, source + k) for source in range(4 - k)])
        for k in (1, 2, 3)
    ]
    attended = merge(x.reshape(1), received)
    returned = lax.all_to_all(attended, HEAD_AXES, split_axis=0, concat_axis=0, tiled=True)
    first = ((x == 0) & (lax.axis_index("zh") == 0)).astype(jnp.int32).reshape(1)
    return tuple(
        finish(
            noise_level, first, returned, latent, latent_before, entering, gate_table
        )
    )


def solution(mesh):
    fine = Mesh(mesh.devices.reshape(4, 4, 4, 4, 2), ("x", "zh", "zl", "y", "c"))
    section, seq = ("x", "zh"), ("zl", "y", "c")
    placed = (
        P(section, seq, None),
        P(section, seq, None),
        P(section, seq, None),
        P(section, seq, None),
        P(seq, None),
        P(section),
        P(),
        P(),
        P(),
    )
    return jax.shard_map(
        local,
        mesh=fine,
        in_specs=placed,
        out_specs=(P(section, seq, None), P(section, seq, None)),
        check_vma=False,
    )
```

```python
import math

import jax
import jax.numpy as jnp
from jax import lax
from jax.experimental import pallas as pl
from jax.experimental.pallas import tpu as pltpu
from jax.sharding import Mesh
from jax.sharding import PartitionSpec as P

HD = 128
HEADS = 32
ROWS = 24
QUARTER = 192
BLOCK = 768
STAT = 16
LANES = 256
SCALE = math.log2(math.e) / math.sqrt(HD)
LOW = -1e30
f32 = jnp.float32
bf16 = jnp.bfloat16

VM = pl.BlockSpec(memory_space=pltpu.VMEM)
SM = pl.BlockSpec(memory_space=pltpu.SMEM)
PARAMS = pltpu.CompilerParams(vmem_limit_bytes=48 * 2**20)
HEAD_AXES = ("zh", "zl", "c")


def pack_kernel(level_ref, q_hbm, k_hbm, v_hbm, latent_hbm, o_ref, latent_ref, buf, sems):
    sources = (q_hbm, k_hbm, v_hbm, latent_hbm)
    copies = [pltpu.make_async_copy(ref, buf.at[i], sems.at[i]) for i, ref in enumerate(sources)]
    for copy in copies:
        copy.start()
    latent_ref[0, :, HEADS * HD :] = jnp.full((ROWS, HD), level_ref[0], jnp.int32).astype(
        f32
    ).astype(bf16)
    for i in range(3):
        copies[i].wait()
        for h in range(HEADS):
            o_ref[h, i] = buf[i, 0, :, h * HD : (h + 1) * HD]
    copies[3].wait()
    latent_ref[0, :, : HEADS * HD] = buf[3, 0]


def pack(level, queries, keys, values, latent):
    hbm = pl.BlockSpec(memory_space=pltpu.HBM)
    return pl.pallas_call(
        pack_kernel,
        out_shape=[
            jax.ShapeDtypeStruct((HEADS, 3, ROWS, HD), bf16),
            jax.ShapeDtypeStruct((1, ROWS, HEADS * HD + HD), bf16),
        ],
        in_specs=[SM] + [hbm] * 4,
        out_specs=[VM] * 2,
        scratch_shapes=[
            pltpu.VMEM((4, 1, ROWS, HEADS * HD), bf16),
            pltpu.SemaphoreType.DMA((4,)),
        ],
        compiler_params=PARAMS,
    )(level, queries, keys, values, latent)


def token_of(shape, dim):
    i = lax.broadcasted_iota(jnp.int32, shape, dim)
    one, nil = jnp.int32(1), jnp.int32(0)
    part = sum(jnp.where(i >= e * QUARTER, one, nil) for e in (1, 2, 3))
    inner = i - part * QUARTER
    run = sum(jnp.where(inner >= e * 48, one, nil) for e in (1, 2, 3))
    return inner + run * (QUARTER - 48) + part * 48


def attend_kernel(
    count_ref, flag_ref, place_ref, kv_ref, q_ref, o0, o1, o2, o3,
    q_sc, k_sc, v_sc, m_sc, acc_sc, s0, s1, units,
):
    def build(e, n):
        slot, t = e // 4, e % 4
        active = flag_ref[slot * 4, t]
        for g in range(1, 4):
            active = active | flag_ref[slot * 4 + g, t]

        @pl.when(active == 1)
        def _():
            units[0, n] = slot
            units[1, n] = t

        return n + active

    for i in range(2):
        units[0, i] = 4
        units[1, i] = 0
    n = lax.fori_loop(0, 16, build, jnp.int32(2))
    for i in range(4):
        units[0, n + i] = 4
        units[1, n + i] = 0

    for slot in range(4):
        q_sc[slot] = q_ref[jnp.minimum(place_ref[0] + slot, 3)].reshape(BLOCK, HD)

    token = token_of((BLOCK, HD), 0)
    token_row = token_of((STAT, BLOCK), 1)
    for t in range(4):
        k = jnp.concatenate([kv_ref[y, t, :, 0].reshape(QUARTER, HD) for y in range(4)])
        v = jnp.concatenate([kv_ref[y, t, :, 1].reshape(QUARTER, HD) for y in range(4)])
        valid = token < count_ref[t]
        k_sc[t] = jnp.where(valid, k, jnp.broadcast_to(k[0:1], k.shape))
        v_sc[t, :HD] = jnp.where(valid, v, jnp.zeros_like(v)).T
        v_sc[t, HD:] = jnp.where(token_row < count_ref[t], 1.0, 0.0).astype(bf16)

    m_sc[...] = jnp.full(m_sc.shape, LOW, f32)
    acc_sc[...] = jnp.zeros(acc_sc.shape, f32)
    lane = lax.broadcasted_iota(jnp.int32, (8, LANES), 1)

    def unit(i, j, s_read, s_write):
        span = slice(j * LANES, (j + 1) * LANES)
        slot, t = units[0, i], units[1, i]
        first = jnp.minimum(slot, 3) * 4
        flag = jnp.full((8, LANES), flag_ref[first + (j * LANES) // QUARTER, t], jnp.int32)
        for g in range(1, 4):
            if j * LANES < g * QUARTER < (j + 1) * LANES:
                flag = jnp.where(lane + j * LANES >= g * QUARTER, flag_ref[first + g, t], flag)
        on = flag == 1
        old = m_sc[slot, :, span]
        top = jnp.max(s_read[:, span], axis=0, keepdims=True) * SCALE
        new = jnp.where(on, jnp.maximum(old, top), old)
        m_sc[slot, :, span] = new
        a = jnp.exp2(old - new)
        p = jnp.exp2(s_read[:, span] * SCALE - jnp.where(on, new, -LOW)[:1]).astype(bf16)
        score(i + 1, span, s_write)
        part = jnp.dot(v_sc[t], p, preferred_element_type=f32)
        acc_sc[slot, :, span] = acc_sc[slot, :, span] * a[:1] + part

    def score(i, span, s):
        slot = jnp.minimum(units[0, i], 3)
        s[:, span] = lax.dot_general(
            k_sc[units[1, i]], q_sc[slot, span], (((1,), (1,)), ((), ())), preferred_element_type=f32
        )

    def step(h, carry):
        i = 2 + 2 * h
        for j in range(BLOCK // LANES):
            unit(i, j, s0, s1)
        for j in range(BLOCK // LANES):
            unit(i + 1, j, s1, s0)
        return carry

    for j in range(BLOCK // LANES):
        score(2, slice(j * LANES, (j + 1) * LANES), s0)
    lax.fori_loop(0, (n - 1) // 2, step, 0)

    outs = (o0, o1, o2, o3)
    for slot in range(4):
        total = acc_sc[slot, HD : HD + 1]
        some = total > 0.0
        safe = jnp.where(some, total, 1.0)
        head = (acc_sc[slot, :HD] * (1.0 / safe)).astype(bf16)
        level = jnp.where(some, m_sc[slot, :1] + jnp.log2(safe), LOW)
        hi = level.astype(bf16)
        mid = (level - hi.astype(f32)).astype(bf16)
        lo = (level - hi.astype(f32) - mid.astype(f32)).astype(bf16)
        stat = jnp.concatenate([hi, mid, lo, jnp.zeros((STAT - 3, BLOCK), bf16)], axis=0)
        outs[slot][:HD, :BLOCK] = head
        outs[slot][HD:, :BLOCK] = stat
        if slot < 3:
            outs[slot + 1][:HD, BLOCK:] = head[:, BLOCK - QUARTER :]
            outs[slot + 1][HD:, BLOCK:] = stat[:, BLOCK - QUARTER :]


def attend(counts, flags, place, q, kv):
    vmem = pltpu.VMEM
    return pl.pallas_call(
        attend_kernel,
        out_shape=[
            jax.ShapeDtypeStruct((HD + STAT, BLOCK + (QUARTER if slot else 0)), bf16)
            for slot in range(4)
        ],
        in_specs=[SM] * 3 + [VM] * 2,
        out_specs=[VM] * 4,
        scratch_shapes=[
            vmem((4, BLOCK, HD), bf16),
            vmem((4, BLOCK, HD), bf16),
            vmem((4, HD + STAT, BLOCK), bf16),
            vmem((5, 8, BLOCK), f32),
            vmem((5, HD + STAT, BLOCK), f32),
            vmem((BLOCK, BLOCK), f32),
            vmem((BLOCK, BLOCK), f32),
            pltpu.SMEM((2, 24), jnp.int32),
        ],
        compiler_params=PARAMS,
        cost_estimate=pl.CostEstimate(
            flops=64 * BLOCK * BLOCK * HD, bytes_accessed=8 << 20, transcendentals=16 * BLOCK * BLOCK
        ),
    )(counts, flags, place, kv, q)


def blend(stats, heads):
    levels = [stat[0:1] + stat[1:2] + stat[2:3] for stat in stats]
    top = levels[0]
    for level in levels[1:]:
        top = jnp.maximum(top, level)
    shares = [jnp.exp2(level - top) for level in levels]
    whole = sum(shares[1:], shares[0])
    total = sum(head.astype(f32) * (share / whole) for head, share in zip(heads, shares))
    return total.T.astype(bf16)


def merge_kernel(x_ref, r0, r1, r2, r3, o_ref):
    stats, heads = [r0[HD:].astype(f32)], [r0[:HD]]
    for k, ref in ((1, r1), (2, r2), (3, r3)):
        stat = ref[HD:].astype(f32)
        row = lax.broadcasted_iota(jnp.int32, stat.shape, 0)
        stats.append(jnp.where(x_ref[0] >= k, stat, jnp.where(row == 0, LOW, 0.0)))
        heads.append(ref[:HD])
    own = blend([stat[:, :BLOCK] for stat in stats], [head[:, :BLOCK] for head in heads])
    tail = blend([stat[:, BLOCK:] for stat in stats[1:]], [head[:, BLOCK:] for head in heads[1:]])
    own = own.reshape(HEADS, ROWS, HD)
    o_ref[:, 0] = own
    o_ref[:8, 1] = tail.reshape(8, ROWS, HD)
    o_ref[8:, 1] = own[: HEADS - 8]


def merge(x, parts):
    return pl.pallas_call(
        merge_kernel,
        out_shape=jax.ShapeDtypeStruct((HEADS, 2, ROWS, HD), bf16),
        in_specs=[SM] + [VM] * 4,
        out_specs=VM,
        compiler_params=PARAMS,
    )(x, *parts)


def finish_kernel(
    level_ref, first_ref, r_ref, latent_ref, latent_before_ref, entering_ref, gate_ref,
    updated_ref, advanced_ref,
):
    def update(which, level, residual):
        squares = jnp.zeros((ROWS, HD), f32)
        for h in range(HEADS):
            wide = r_ref[h, which].astype(f32)
            squares = squares + wide * wide
        mean = jnp.sum(squares, axis=-1, keepdims=True) * (1.0 / (HEADS * HD))
        factor = 1.0 / jnp.sqrt(mean + 1e-06)
        index = lax.broadcasted_iota(jnp.int32, (gate_ref.shape[0], HD), 0)
        mine = index.astype(f32) == level
        for h in range(HEADS):
            span = slice(h * HD, (h + 1) * HD)
            gate = jnp.sum(jnp.where(mine, gate_ref[:, span], 0.0), axis=0, keepdims=True)
            wide = r_ref[h, which].astype(f32)
            yield span, residual[0, :, span].astype(f32) + gate * (wide * factor)

    for span, value in update(0, level_ref[0].astype(f32), latent_ref):
        updated_ref[0, :, span] = value.astype(bf16)
    first = first_ref[0] == 1
    before = latent_before_ref[0, :1, HEADS * HD :].astype(f32)
    for span, value in update(1, before, latent_before_ref):
        advanced_ref[0, :, span] = jnp.where(first, entering_ref[:, span], value.astype(bf16))


def finish(level, first, returned, latent, latent_before, entering, gate_table):
    return pl.pallas_call(
        finish_kernel,
        out_shape=[jax.ShapeDtypeStruct(latent.shape, bf16)] * 2,
        in_specs=[SM] * 2 + [VM] * 5,
        out_specs=[VM] * 2,
        compiler_params=PARAMS,
    )(level, first, returned, latent, latent_before, entering, gate_table)


def local(
    queries, keys, values, latent, entering, noise_level, token_counts, block_mask, gate_table
):
    x = lax.axis_index("x")
    queries, keys, values, latent_in = (pltpu.with_memory_space_constraint(a, pltpu.HBM) for a in (queries, keys, values, latent))
    packed, latent_level = pack(noise_level, queries, keys, values, latent_in)
    packed = lax.all_to_all(packed, HEAD_AXES, split_axis=0, concat_axis=0, tiled=True)
    packed, latent_level = lax.optimization_barrier((packed, latent_level))
    kv = packed[:, 1:3].reshape(4, 8, 2, ROWS, HD)
    kv, packed = lax.optimization_barrier((kv, packed))
    q = lax.all_gather(packed[:, 0], "x", axis=0, tiled=False)
    kv = jnp.broadcast_to(kv[None], (4, *kv.shape))
    kv = lax.all_to_all(kv, "y", split_axis=0, concat_axis=0, tiled=True)
    onward = [(s, s + 1) for s in range(15)]
    latent_before = lax.ppermute(latent_level, ("x", "zh"), onward)
    padded = jnp.concatenate([block_mask, jnp.zeros_like(block_mask)], axis=0)
    flags = lax.dynamic_slice(padded, (4 * x, 4 * x), (16, 4))
    counts = lax.dynamic_slice(token_counts, (4 * x,), (4,))
    parts = attend(counts, flags, x.reshape(1), q, kv)
    parts, latent_before = lax.optimization_barrier((parts, latent_before))
    received = [parts[0]] + [
        lax.ppermute(parts[k], "x", [(source, source + k) for source in range(4 - k)])
        for k in (1, 2, 3)
    ]
    attended = merge(x.reshape(1), received)
    returned = lax.all_to_all(attended, HEAD_AXES, split_axis=0, concat_axis=0, tiled=True)
    first = ((x == 0) & (lax.axis_index("zh") == 0)).astype(jnp.int32).reshape(1)
    return tuple(
        finish(
            noise_level, first, returned, latent, latent_before, entering, gate_table
        )
    )


def solution(mesh):
    fine = Mesh(mesh.devices.reshape(4, 4, 4, 4, 2), ("x", "zh", "zl", "y", "c"))
    section, seq = ("x", "zh"), ("zl", "y", "c")
    placed = (
        P(section, seq, None),
        P(section, seq, None),
        P(section, seq, None),
        P(section, seq, None),
        P(seq, None),
        P(section),
        P(),
        P(),
        P(),
    )
    return jax.shard_map(
        local,
        mesh=fine,
        in_specs=placed,
        out_specs=(P(section, seq, None), P(section, seq, None)),
        check_vma=False,
    )
```

```python
import math

import jax
import jax.numpy as jnp
from jax import lax
from jax.experimental import pallas as pl
from jax.experimental.pallas import tpu as pltpu
from jax.sharding import Mesh
from jax.sharding import PartitionSpec as P

HD = 128
HEADS = 32
ROWS = 24
QUARTER = 192
BLOCK = 768
STAT = 16
SENT = 8
LANES = 256
SCALE = math.log2(math.e) / math.sqrt(HD)
LOW = -1e30
f32 = jnp.float32
bf16 = jnp.bfloat16

VM = pl.BlockSpec(memory_space=pltpu.VMEM)
SM = pl.BlockSpec(memory_space=pltpu.SMEM)
PARAMS = pltpu.CompilerParams(vmem_limit_bytes=48 * 2**20)
HEAD_AXES = ("zh", "zl", "c")


def pack_kernel(level_ref, q_hbm, k_hbm, v_hbm, latent_hbm, o_ref, latent_ref, buf, sems):
    sources = (q_hbm, k_hbm, v_hbm, latent_hbm)
    copies = [pltpu.make_async_copy(ref, buf.at[i], sems.at[i]) for i, ref in enumerate(sources)]
    for copy in copies:
        copy.start()
    latent_ref[0, :, HEADS * HD :] = jnp.full((ROWS, HD), level_ref[0], jnp.int32).astype(
        f32
    ).astype(bf16)
    for i in range(3):
        copies[i].wait()
        for h in range(HEADS):
            o_ref[h, i] = buf[i, 0, :, h * HD : (h + 1) * HD]
    copies[3].wait()
    latent_ref[0, :, : HEADS * HD] = buf[3, 0]


def pack(level, queries, keys, values, latent):
    hbm = pl.BlockSpec(memory_space=pltpu.HBM)
    return pl.pallas_call(
        pack_kernel,
        out_shape=[
            jax.ShapeDtypeStruct((HEADS, 3, ROWS, HD), bf16),
            jax.ShapeDtypeStruct((1, ROWS, HEADS * HD + HD), bf16),
        ],
        in_specs=[SM] + [hbm] * 4,
        out_specs=[VM] * 2,
        scratch_shapes=[
            pltpu.VMEM((4, 1, ROWS, HEADS * HD), bf16),
            pltpu.SemaphoreType.DMA((4,)),
        ],
        compiler_params=PARAMS,
    )(level, queries, keys, values, latent)


def unpack_kernel(packed_ref, q_ref, kv_ref):
    q_ref[...] = packed_ref[:, 0]
    for copy in range(4):
        kv_ref[copy] = packed_ref[:, 1:]


def unpack(packed):
    return pl.pallas_call(
        unpack_kernel,
        out_shape=[
            jax.ShapeDtypeStruct((HEADS, ROWS, HD), bf16),
            jax.ShapeDtypeStruct((4, HEADS, 2, ROWS, HD), bf16),
        ],
        in_specs=[VM],
        out_specs=[VM] * 2,
        compiler_params=PARAMS,
    )(packed)


def token_of(shape, dim):
    i = lax.broadcasted_iota(jnp.int32, shape, dim)
    one, nil = jnp.int32(1), jnp.int32(0)
    part = sum(jnp.where(i >= e * QUARTER, one, nil) for e in (1, 2, 3))
    inner = i - part * QUARTER
    run = sum(jnp.where(inner >= e * 48, one, nil) for e in (1, 2, 3))
    return inner + run * (QUARTER - 48) + part * 48


def list_units(units, flag_ref, slots, dummy):
    def build(e, n):
        slot, t = slots[0] + e // 4, e % 4
        active = flag_ref[slot * 4, t]
        for g in range(1, 4):
            active = active | flag_ref[slot * 4 + g, t]

        @pl.when(active == 1)
        def _():
            units[0, n] = slot
            units[1, n] = t

        return n + active

    n = lax.fori_loop(0, 4 * len(slots), build, jnp.int32(0))
    for i in range(2):
        units[0, n + i] = dummy
        units[1, n + i] = 0
    return n


def run_units(units, steps, flag_ref, q_sc, k_ref, v_ref, m_sc, acc_sc, s0, s1):
    real = q_sc.shape[0]
    lane = lax.broadcasted_iota(jnp.int32, (8, LANES), 1)

    def score(i, j, s):
        span = slice(j * LANES, (j + 1) * LANES)
        slot = jnp.minimum(units[0, i], real - 1)
        s[:, span] = lax.dot_general(
            k_ref[units[1, i]], q_sc[slot, span], (((1,), (1,)), ((), ())), preferred_element_type=f32
        )

    def weigh(i, j, s_read, s_write):
        span = slice(j * LANES, (j + 1) * LANES)
        slot, t = units[0, i], units[1, i]
        first = jnp.minimum(slot, real - 1) * 4
        flag = jnp.full((8, LANES), flag_ref[first + (j * LANES) // QUARTER, t], jnp.int32)
        for g in range(1, 4):
            if j * LANES < g * QUARTER < (j + 1) * LANES:
                flag = jnp.where(lane + j * LANES >= g * QUARTER, flag_ref[first + g, t], flag)
        on = flag == 1
        old = m_sc[slot, :, span]
        top = jnp.max(s_read[:, span], axis=0, keepdims=True) * SCALE
        new = jnp.where(on, jnp.maximum(old, top), old)
        m_sc[slot, :, span] = new
        a = jnp.exp2(old - new)
        p = jnp.exp2(s_read[:, span] * SCALE - jnp.where(on, new, -LOW)[:1]).astype(bf16)
        score(i + 1, j, s_write)
        part = jnp.dot(v_ref[t], p, preferred_element_type=f32)
        acc_sc[slot, :, span] = acc_sc[slot, :, span] * a[:1] + part

    def pair(h, carry):
        for j in steps:
            weigh(2 * h, j, s0, s1)
        for j in steps:
            weigh(2 * h + 1, j, s1, s0)
        return carry

    def run(n):
        for j in steps:
            score(0, j, s0)
        lax.fori_loop(0, (n + 1) // 2, pair, 0)

    return run


def partial(m, acc):
    total = acc[HD : HD + 1]
    some = total > 0.0
    safe = jnp.where(some, total, 1.0)
    level = jnp.where(some, m[:1] + jnp.log2(safe), LOW)
    hi = level.astype(bf16)
    mid = (level - hi.astype(f32)).astype(bf16)
    lo = (level - hi.astype(f32) - mid.astype(f32)).astype(bf16)
    stat = jnp.concatenate([hi, mid, lo, jnp.zeros((SENT - 3, level.shape[1]), bf16)], axis=0)
    return (acc[:HD] * (1.0 / safe)).astype(bf16), stat


def put(ref, span, part):
    head, stat = part
    ref[:HD, span] = head
    ref[HD:, span] = stat


def outer_kernel(
    count_ref, flag_ref, place_ref, kv_ref, q_ref, o0, o1, o2, o3, k_ref, v_ref,
    q_sc, m_sc, acc_sc, s0, s1, units,
):
    for slot in range(4):
        q_sc[slot] = q_ref[jnp.minimum(place_ref[0] + slot, 3)].reshape(BLOCK, HD)

    token = token_of((BLOCK, HD), 0)
    token_row = token_of((STAT, BLOCK), 1)
    for t in range(4):
        k = jnp.concatenate([kv_ref[y, t, :, 0].reshape(QUARTER, HD) for y in range(4)])
        v = jnp.concatenate([kv_ref[y, t, :, 1].reshape(QUARTER, HD) for y in range(4)])
        valid = token < count_ref[t]
        k_ref[t] = jnp.where(valid, k, jnp.broadcast_to(k[0:1], k.shape))
        v_ref[t, :HD] = jnp.where(valid, v, jnp.zeros_like(v)).T
        v_ref[t, HD:] = jnp.where(token_row < count_ref[t], 1.0, 0.0).astype(bf16)

    m_sc[...] = jnp.full(m_sc.shape, LOW, f32)
    acc_sc[...] = jnp.zeros(acc_sc.shape, f32)
    refs = (flag_ref, q_sc, k_ref, v_ref, m_sc, acc_sc, s0, s1)
    run_units(units, (0, 1, 2), *refs)(list_units(units, flag_ref, (1, 2, 3), 4))
    run_units(units, (2,), *refs)(list_units(units, flag_ref, (0,), 4))

    last = BLOCK - LANES
    own = partial(m_sc[0, :, last:], acc_sc[0, :, last:])
    put(o0, slice(0, LANES), own)
    before = [piece[:, LANES - QUARTER :] for piece in own]
    for slot, ref in ((1, o1), (2, o2), (3, o3)):
        part = partial(m_sc[slot], acc_sc[slot])
        put(ref, slice(0, BLOCK), part)
        put(ref, slice(BLOCK, BLOCK + QUARTER), before)
        before = [piece[:, BLOCK - QUARTER :] for piece in part]


def own_kernel(
    flag_ref, place_ref, q_ref, k_ref, v_ref, o_ref, q_sc, m_sc, acc_sc, s0, s1, units
):
    q_sc[0] = q_ref[place_ref[0]].reshape(BLOCK, HD)
    m_sc[...] = jnp.full(m_sc.shape, LOW, f32)
    acc_sc[...] = jnp.zeros(acc_sc.shape, f32)
    refs = (flag_ref, q_sc, k_ref, v_ref, m_sc, acc_sc, s0, s1)
    run_units(units, (0, 1), *refs)(list_units(units, flag_ref, (0,), 1))
    rest = BLOCK - LANES
    put(o_ref, slice(0, rest), partial(m_sc[0, :, :rest], acc_sc[0, :, :rest]))


def scratch(slots):
    vmem = pltpu.VMEM
    return [
        vmem((slots, BLOCK, HD), bf16),
        vmem((slots + 1, 8, BLOCK), f32),
        vmem((slots + 1, HD + STAT, BLOCK), f32),
        vmem((BLOCK, BLOCK), f32),
        vmem((BLOCK, BLOCK), f32),
        pltpu.SMEM((2, 16), jnp.int32),
    ]


def cost(units):
    return pl.CostEstimate(
        flops=4 * units * BLOCK * BLOCK * HD,
        bytes_accessed=8 << 20,
        transcendentals=units * BLOCK * BLOCK,
    )


def attend_outer(counts, flags, place, q, kv):
    return pl.pallas_call(
        outer_kernel,
        out_shape=[
            jax.ShapeDtypeStruct((HD + SENT, columns), bf16)
            for columns in (LANES, BLOCK + QUARTER, BLOCK + QUARTER, BLOCK + QUARTER)
        ]
        + [
            jax.ShapeDtypeStruct((4, BLOCK, HD), bf16),
            jax.ShapeDtypeStruct((4, HD + STAT, BLOCK), bf16),
        ],
        in_specs=[SM] * 3 + [VM] * 2,
        out_specs=[VM] * 6,
        scratch_shapes=scratch(4),
        compiler_params=PARAMS,
        cost_estimate=cost(14),
    )(counts, flags, place, kv, q)


def attend_own(flags, place, q, k, v):
    return pl.pallas_call(
        own_kernel,
        out_shape=jax.ShapeDtypeStruct((HD + SENT, BLOCK - LANES), bf16),
        in_specs=[SM] * 2 + [VM] * 3,
        out_specs=VM,
        scratch_shapes=scratch(1),
        compiler_params=PARAMS,
        cost_estimate=cost(4),
    )(flags, place, q, k, v)


def blend(stats, heads):
    levels = [stat[0:1] + stat[1:2] + stat[2:3] for stat in stats]
    top = levels[0]
    for level in levels[1:]:
        top = jnp.maximum(top, level)
    shares = [jnp.exp2(level - top) for level in levels]
    whole = sum(shares[1:], shares[0])
    total = sum(head.astype(f32) * (share / whole) for head, share in zip(heads, shares))
    return total.T.astype(bf16)


def merge_kernel(x_ref, r0, r0_last, r1, r2, r3, o_ref):
    own = jnp.concatenate([r0[...], r0_last[...]], axis=1)
    stats, heads = [own[HD:].astype(f32)], [own[:HD]]
    for k, ref in ((1, r1), (2, r2), (3, r3)):
        stat = ref[HD:].astype(f32)
        row = lax.broadcasted_iota(jnp.int32, stat.shape, 0)
        stats.append(jnp.where(x_ref[0] >= k, stat, jnp.where(row == 0, LOW, 0.0)))
        heads.append(ref[:HD])
    own = blend([stat[:, :BLOCK] for stat in stats], [head[:, :BLOCK] for head in heads])
    tail = blend([stat[:, BLOCK:] for stat in stats[1:]], [head[:, BLOCK:] for head in heads[1:]])
    own = own.reshape(HEADS, ROWS, HD)
    o_ref[:, 0] = own
    o_ref[:8, 1] = tail.reshape(8, ROWS, HD)
    o_ref[8:, 1] = own[: HEADS - 8]


def merge(x, parts):
    return pl.pallas_call(
        merge_kernel,
        out_shape=jax.ShapeDtypeStruct((HEADS, 2, ROWS, HD), bf16),
        in_specs=[SM] + [VM] * 5,
        out_specs=VM,
        compiler_params=PARAMS,
    )(x, *parts)


def finish_kernel(
    level_ref, first_ref, r_ref, latent_ref, latent_before_ref, entering_ref, gate_ref,
    updated_ref, advanced_ref,
):
    def update(which, level, residual):
        squares = jnp.zeros((ROWS, HD), f32)
        for h in range(HEADS):
            wide = r_ref[h, which].astype(f32)
            squares = squares + wide * wide
        mean = jnp.sum(squares, axis=-1, keepdims=True) * (1.0 / (HEADS * HD))
        factor = 1.0 / jnp.sqrt(mean + 1e-06)
        index = lax.broadcasted_iota(jnp.int32, (gate_ref.shape[0], HD), 0)
        mine = index.astype(f32) == level
        for h in range(HEADS):
            span = slice(h * HD, (h + 1) * HD)
            gate = jnp.sum(jnp.where(mine, gate_ref[:, span], 0.0), axis=0, keepdims=True)
            wide = r_ref[h, which].astype(f32)
            yield span, residual[0, :, span].astype(f32) + gate * (wide * factor)

    for span, value in update(0, level_ref[0].astype(f32), latent_ref):
        updated_ref[0, :, span] = value.astype(bf16)
    first = first_ref[0] == 1
    before = latent_before_ref[0, :1, HEADS * HD :].astype(f32)
    for span, value in update(1, before, latent_before_ref):
        advanced_ref[0, :, span] = jnp.where(first, entering_ref[:, span], value.astype(bf16))


def finish(level, first, returned, latent, latent_before, entering, gate_table):
    return pl.pallas_call(
        finish_kernel,
        out_shape=[jax.ShapeDtypeStruct(latent.shape, bf16)] * 2,
        in_specs=[SM] * 2 + [VM] * 5,
        out_specs=[VM] * 2,
        compiler_params=PARAMS,
    )(level, first, returned, latent, latent_before, entering, gate_table)


def local(
    queries, keys, values, latent, entering, noise_level, token_counts, block_mask, gate_table
):
    x = lax.axis_index("x")
    sources = [
        pltpu.with_memory_space_constraint(source, pltpu.HBM)
        for source in (queries, keys, values, latent)
    ]
    packed, latent_level = pack(noise_level, *sources)
    packed = lax.all_to_all(packed, HEAD_AXES, split_axis=0, concat_axis=0, tiled=True)
    packed, latent_level = lax.optimization_barrier((packed, latent_level))
    q, kv = unpack(packed)
    q = lax.all_gather(q, "x", axis=0, tiled=False)
    kv = lax.all_to_all(kv, "y", split_axis=0, concat_axis=0, tiled=True)
    kv = kv.reshape(4, 4, 8, 2, ROWS, HD)
    onward = [(s, s + 1) for s in range(15)]
    latent_before = lax.ppermute(latent_level, ("x", "zh"), onward)
    padded = jnp.concatenate([block_mask, jnp.zeros_like(block_mask)], axis=0)
    flags = lax.dynamic_slice(padded, (4 * x, 4 * x), (16, 4))
    counts = lax.dynamic_slice(token_counts, (4 * x,), (4,))
    place = x.reshape(1)
    *parts, k, v = attend_outer(counts, flags, place, q, kv)
    parts, latent_before = lax.optimization_barrier((parts, latent_before))
    received = [
        lax.ppermute(parts[k], "x", [(source, source + k) for source in range(4 - k)])
        for k in (1, 2, 3)
    ]
    own = attend_own(flags, place, q, k, v)
    attended = merge(place, [own, parts[0], *received])
    returned = lax.all_to_all(attended, HEAD_AXES, split_axis=0, concat_axis=0, tiled=True)
    first = ((x == 0) & (lax.axis_index("zh") == 0)).astype(jnp.int32).reshape(1)
    return tuple(
        finish(
            noise_level, first, returned, latent, latent_before, entering, gate_table
        )
    )


def solution(mesh):
    fine = Mesh(mesh.devices.reshape(4, 4, 4, 4, 2), ("x", "zh", "zl", "y", "c"))
    section, seq = ("x", "zh"), ("zl", "y", "c")
    placed = (
        P(section, seq, None),
        P(section, seq, None),
        P(section, seq, None),
        P(section, seq, None),
        P(seq, None),
        P(section),
        P(),
        P(),
        P(),
    )
    return jax.shard_map(
        local,
        mesh=fine,
        in_specs=placed,
        out_specs=(P(section, seq, None), P(section, seq, None)),
        check_vma=False,
    )
```

```python
import math

import jax
import jax.numpy as jnp
from jax import lax
from jax.experimental import pallas as pl
from jax.experimental.pallas import tpu as pltpu
from jax.sharding import Mesh
from jax.sharding import PartitionSpec as P

HD = 128
HEADS = 32
ROWS = 24
QUARTER = 192
BLOCK = 768
STAT = 16
SENT = 8
LANES = 256
SCALE = math.log2(math.e) / math.sqrt(HD)
LOW = -1e30
f32 = jnp.float32
bf16 = jnp.bfloat16

VM = pl.BlockSpec(memory_space=pltpu.VMEM)
SM = pl.BlockSpec(memory_space=pltpu.SMEM)
PARAMS = pltpu.CompilerParams(vmem_limit_bytes=48 * 2**20)
HEAD_AXES = ("zh", "zl", "c")


def pack_kernel(level_ref, q_hbm, k_hbm, v_hbm, latent_hbm, o_ref, latent_ref, buf, sems):
    sources = (q_hbm, k_hbm, v_hbm, latent_hbm)
    copies = [pltpu.make_async_copy(ref, buf.at[i], sems.at[i]) for i, ref in enumerate(sources)]
    for copy in copies:
        copy.start()
    latent_ref[0, :, HEADS * HD :] = jnp.full((ROWS, HD), level_ref[0], jnp.int32).astype(
        f32
    ).astype(bf16)
    for i in range(3):
        copies[i].wait()
        for h in range(HEADS):
            o_ref[h, i] = buf[i, 0, :, h * HD : (h + 1) * HD]
    copies[3].wait()
    latent_ref[0, :, : HEADS * HD] = buf[3, 0]


def pack(level, queries, keys, values, latent):
    hbm = pl.BlockSpec(memory_space=pltpu.HBM)
    return pl.pallas_call(
        pack_kernel,
        out_shape=[
            jax.ShapeDtypeStruct((HEADS, 3, ROWS, HD), bf16),
            jax.ShapeDtypeStruct((1, ROWS, HEADS * HD + HD), bf16),
        ],
        in_specs=[SM] + [hbm] * 4,
        out_specs=[VM] * 2,
        scratch_shapes=[
            pltpu.VMEM((4, 1, ROWS, HEADS * HD), bf16),
            pltpu.SemaphoreType.DMA((4,)),
        ],
        compiler_params=PARAMS,
    )(level, queries, keys, values, latent)


def unpack_kernel(packed_ref, q_ref, kv_ref):
    q_ref[...] = packed_ref[:, 0]
    for copy in range(4):
        kv_ref[copy] = packed_ref[:, 1:]


def unpack(packed):
    return pl.pallas_call(
        unpack_kernel,
        out_shape=[
            jax.ShapeDtypeStruct((HEADS, ROWS, HD), bf16),
            jax.ShapeDtypeStruct((4, HEADS, 2, ROWS, HD), bf16),
        ],
        in_specs=[VM],
        out_specs=[VM] * 2,
        compiler_params=PARAMS,
    )(packed)


def token_of(shape, dim):
    i = lax.broadcasted_iota(jnp.int32, shape, dim)
    one, nil = jnp.int32(1), jnp.int32(0)
    part = sum(jnp.where(i >= e * QUARTER, one, nil) for e in (1, 2, 3))
    inner = i - part * QUARTER
    run = sum(jnp.where(inner >= e * 48, one, nil) for e in (1, 2, 3))
    return inner + run * (QUARTER - 48) + part * 48


def list_units(units, flag_ref, slots, dummy):
    def build(e, n):
        slot, t = slots[0] + e // 4, e % 4
        active = flag_ref[slot * 4, t]
        for g in range(1, 4):
            active = active | flag_ref[slot * 4 + g, t]

        @pl.when(active == 1)
        def _():
            units[0, n] = slot
            units[1, n] = t

        return n + active

    n = lax.fori_loop(0, 4 * len(slots), build, jnp.int32(0))
    for i in range(2):
        units[0, n + i] = dummy
        units[1, n + i] = 0
    return n


def run_units(units, steps, flag_ref, q_sc, k_ref, v_ref, m_sc, acc_sc, s0, s1):
    real = q_sc.shape[0]
    lane = lax.broadcasted_iota(jnp.int32, (8, LANES), 1)

    def score(i, j, s):
        span = slice(j * LANES, (j + 1) * LANES)
        slot = jnp.minimum(units[0, i], real - 1)
        s[:, span] = lax.dot_general(
            k_ref[units[1, i]], q_sc[slot, span], (((1,), (1,)), ((), ())), preferred_element_type=f32
        )

    def weigh(i, j, s_read, s_write):
        span = slice(j * LANES, (j + 1) * LANES)
        slot, t = units[0, i], units[1, i]
        first = jnp.minimum(slot, real - 1) * 4
        flag = jnp.full((8, LANES), flag_ref[first + (j * LANES) // QUARTER, t], jnp.int32)
        for g in range(1, 4):
            if j * LANES < g * QUARTER < (j + 1) * LANES:
                flag = jnp.where(lane + j * LANES >= g * QUARTER, flag_ref[first + g, t], flag)
        on = flag == 1
        old = m_sc[slot, :, span]
        top = jnp.max(s_read[:, span], axis=0, keepdims=True) * SCALE
        new = jnp.where(on, jnp.maximum(old, top), old)
        m_sc[slot, :, span] = new
        a = jnp.exp2(old - new)
        p = jnp.exp2(s_read[:, span] * SCALE - jnp.where(on, new, -LOW)[:1]).astype(bf16)
        score(i + 1, j, s_write)
        part = jnp.dot(v_ref[t], p, preferred_element_type=f32)
        acc_sc[slot, :, span] = acc_sc[slot, :, span] * a[:1] + part

    def pair(h, carry):
        for j in steps:
            weigh(2 * h, j, s0, s1)
        for j in steps:
            weigh(2 * h + 1, j, s1, s0)
        return carry

    def run(n):
        for j in steps:
            score(0, j, s0)
        lax.fori_loop(0, (n + 1) // 2, pair, 0)

    return run


def clear(m_sc, acc_sc):
    m_sc[...] = jnp.full(m_sc.shape, LOW, f32)
    acc_sc[...] = jnp.zeros(acc_sc.shape, f32)


def partial(m, acc):
    total = acc[HD : HD + 1]
    some = total > 0.0
    safe = jnp.where(some, total, 1.0)
    level = jnp.where(some, m[:1] + jnp.log2(safe), LOW)
    hi = level.astype(bf16)
    mid = (level - hi.astype(f32)).astype(bf16)
    lo = (level - hi.astype(f32) - mid.astype(f32)).astype(bf16)
    stat = jnp.concatenate([hi, mid, lo, jnp.zeros((SENT - 3, level.shape[1]), bf16)], axis=0)
    return (acc[:HD] * (1.0 / safe)).astype(bf16), stat


def put(ref, span, part):
    head, stat = part
    ref[:HD, span] = head
    ref[HD:, span] = stat


def far_kernel(
    count_ref, flag_ref, place_ref, kv_ref, q_ref, o1_last, o2, o3, k_ref, v_ref,
    q_sc, m_sc, acc_sc, s0, s1, units,
):
    for slot in range(1, 4):
        q_sc[slot] = q_ref[jnp.minimum(place_ref[0] + slot, 3)].reshape(BLOCK, HD)

    token = token_of((BLOCK, HD), 0)
    token_row = token_of((STAT, BLOCK), 1)
    for t in range(4):
        k = jnp.concatenate([kv_ref[y, t, :, 0].reshape(QUARTER, HD) for y in range(4)])
        v = jnp.concatenate([kv_ref[y, t, :, 1].reshape(QUARTER, HD) for y in range(4)])
        valid = token < count_ref[t]
        k_ref[t] = jnp.where(valid, k, jnp.broadcast_to(k[0:1], k.shape))
        v_ref[t, :HD] = jnp.where(valid, v, jnp.zeros_like(v)).T
        v_ref[t, HD:] = jnp.where(token_row < count_ref[t], 1.0, 0.0).astype(bf16)

    clear(m_sc, acc_sc)
    refs = (flag_ref, q_sc, k_ref, v_ref, m_sc, acc_sc, s0, s1)
    run_units(units, (0, 1, 2), *refs)(list_units(units, flag_ref, (2, 3), 4))
    run_units(units, (2,), *refs)(list_units(units, flag_ref, (1,), 4))

    last = BLOCK - LANES
    part = partial(m_sc[1, :, last:], acc_sc[1, :, last:])
    put(o1_last, slice(0, LANES), part)
    for slot, ref in ((2, o2), (3, o3)):
        put(ref, slice(BLOCK, BLOCK + QUARTER), [piece[:, -QUARTER:] for piece in part])
        part = partial(m_sc[slot], acc_sc[slot])
        put(ref, slice(0, BLOCK), part)


def attend_rest(out_ref, units, flag_ref, q_sc, k_ref, v_ref, m_sc, acc_sc, s0, s1):
    dummy = q_sc.shape[0]
    refs = (flag_ref, q_sc, k_ref, v_ref, m_sc, acc_sc, s0, s1)
    run_units(units, (0, 1), *refs)(list_units(units, flag_ref, (0,), dummy))
    rest = BLOCK - LANES
    put(out_ref, slice(0, rest), partial(m_sc[0, :, :rest], acc_sc[0, :, :rest]))


def next_kernel(
    flag_ref, place_ref, q_ref, k_ref, v_ref, o1_last, o0_last, o0_rest, o1,
    q_sc, m_sc, acc_sc, s0, s1, units,
):
    for slot in range(2):
        q_sc[slot] = q_ref[jnp.minimum(place_ref[0] + slot, 3)].reshape(BLOCK, HD)
    clear(m_sc, acc_sc)
    refs = (flag_ref, q_sc, k_ref, v_ref, m_sc, acc_sc, s0, s1)
    run_units(units, (0, 1), *refs)(list_units(units, flag_ref, (1,), 2))
    run_units(units, (2,), *refs)(list_units(units, flag_ref, (0,), 2))
    last = BLOCK - LANES
    put(o1, slice(0, last), partial(m_sc[1, :, :last], acc_sc[1, :, :last]))
    o1[:, last:BLOCK] = o1_last[...]
    part = partial(m_sc[0, :, last:], acc_sc[0, :, last:])
    put(o0_last, slice(0, LANES), part)
    put(o1, slice(BLOCK, BLOCK + QUARTER), [piece[:, -QUARTER:] for piece in part])

    @pl.when(place_ref[0] >= 2)
    def _():
        attend_rest(o0_rest, units, *refs)

    @pl.when(place_ref[0] < 2)
    def _():
        o0_rest[...] = jnp.zeros(o0_rest.shape, bf16)


def own_kernel(
    flag_ref, place_ref, q_ref, k_ref, v_ref, rest_ref, o_ref, q_sc, m_sc, acc_sc, s0, s1, units
):
    @pl.when(place_ref[0] >= 2)
    def _():
        o_ref[...] = rest_ref[...]

    @pl.when(place_ref[0] < 2)
    def _():
        q_sc[0] = q_ref[place_ref[0]].reshape(BLOCK, HD)
        clear(m_sc, acc_sc)
        attend_rest(o_ref, units, flag_ref, q_sc, k_ref, v_ref, m_sc, acc_sc, s0, s1)


def scratch(slots):
    vmem = pltpu.VMEM
    return [
        vmem((slots, BLOCK, HD), bf16),
        vmem((slots + 1, 8, BLOCK), f32),
        vmem((slots + 1, HD + STAT, BLOCK), f32),
        vmem((BLOCK, BLOCK), f32),
        vmem((BLOCK, BLOCK), f32),
        pltpu.SMEM((2, 16), jnp.int32),
    ]


def cost(units):
    return pl.CostEstimate(
        flops=4 * units * BLOCK * BLOCK * HD,
        bytes_accessed=8 << 20,
        transcendentals=units * BLOCK * BLOCK,
    )


def result(columns):
    return jax.ShapeDtypeStruct((HD + SENT, columns), bf16)


def attend_far(counts, flags, place, q, kv):
    return pl.pallas_call(
        far_kernel,
        out_shape=[
            result(LANES),
            result(BLOCK + QUARTER),
            result(BLOCK + QUARTER),
            jax.ShapeDtypeStruct((4, BLOCK, HD), bf16),
            jax.ShapeDtypeStruct((4, HD + STAT, BLOCK), bf16),
        ],
        in_specs=[SM] * 3 + [VM] * 2,
        out_specs=[VM] * 5,
        scratch_shapes=scratch(4),
        compiler_params=PARAMS,
        cost_estimate=cost(10),
    )(counts, flags, place, kv, q)


def attend_next(flags, place, q, k, v, last):
    return pl.pallas_call(
        next_kernel,
        out_shape=[result(LANES), result(BLOCK - LANES), result(BLOCK + QUARTER)],
        in_specs=[SM] * 2 + [VM] * 4,
        out_specs=[VM] * 3,
        scratch_shapes=scratch(2),
        compiler_params=PARAMS,
        cost_estimate=cost(4),
    )(flags, place, q, k, v, last)


def attend_own(flags, place, q, k, v, rest):
    return pl.pallas_call(
        own_kernel,
        out_shape=result(BLOCK - LANES),
        in_specs=[SM] * 2 + [VM] * 4,
        out_specs=VM,
        scratch_shapes=scratch(1),
        compiler_params=PARAMS,
        cost_estimate=cost(4),
    )(flags, place, q, k, v, rest)


def blend(stats, heads):
    levels = [stat[0:1] + stat[1:2] + stat[2:3] for stat in stats]
    top = levels[0]
    for level in levels[1:]:
        top = jnp.maximum(top, level)
    shares = [jnp.exp2(level - top) for level in levels]
    whole = sum(shares[1:], shares[0])
    total = sum(head.astype(f32) * (share / whole) for head, share in zip(heads, shares))
    return total.astype(bf16).T


def merge_kernel(x_ref, r0, r0_last, r1, r2, r3, o_ref):
    own = jnp.concatenate([r0[...], r0_last[...]], axis=1)
    stats, heads = [own[HD:].astype(f32)], [own[:HD]]
    for k, ref in ((1, r1), (2, r2), (3, r3)):
        stat = ref[HD:].astype(f32)
        row = lax.broadcasted_iota(jnp.int32, stat.shape, 0)
        stats.append(jnp.where(x_ref[0] >= k, stat, jnp.where(row == 0, LOW, 0.0)))
        heads.append(ref[:HD])
    own = blend([stat[:, :BLOCK] for stat in stats], [head[:, :BLOCK] for head in heads])
    tail = blend([stat[:, BLOCK:] for stat in stats[1:]], [head[:, BLOCK:] for head in heads[1:]])
    own = own.reshape(HEADS, ROWS, HD)
    o_ref[:, 0] = own
    o_ref[:8, 1] = tail.reshape(8, ROWS, HD)
    o_ref[8:, 1] = own[: HEADS - 8]


def merge(x, parts):
    return pl.pallas_call(
        merge_kernel,
        out_shape=jax.ShapeDtypeStruct((HEADS, 2, ROWS, HD), bf16),
        in_specs=[SM] + [VM] * 5,
        out_specs=VM,
        compiler_params=PARAMS,
    )(x, *parts)


def finish_kernel(
    level_ref, first_ref, r_ref, latent_ref, latent_before_ref, entering_ref, gate_ref,
    updated_ref, advanced_ref,
):
    def update(which, level, residual):
        squares = jnp.zeros((ROWS, HD), f32)
        for h in range(HEADS):
            wide = r_ref[h, which].astype(f32)
            squares = squares + wide * wide
        mean = jnp.sum(squares, axis=-1, keepdims=True) * (1.0 / (HEADS * HD))
        factor = 1.0 / jnp.sqrt(mean + 1e-06)
        index = lax.broadcasted_iota(jnp.int32, (gate_ref.shape[0], HD), 0)
        mine = index.astype(f32) == level
        for h in range(HEADS):
            span = slice(h * HD, (h + 1) * HD)
            gate = jnp.sum(jnp.where(mine, gate_ref[:, span], 0.0), axis=0, keepdims=True)
            wide = r_ref[h, which].astype(f32)
            yield span, residual[0, :, span].astype(f32) + gate * (wide * factor)

    for span, value in update(0, level_ref[0].astype(f32), latent_ref):
        updated_ref[0, :, span] = value.astype(bf16)
    first = first_ref[0] == 1
    before = latent_before_ref[0, :1, HEADS * HD :].astype(f32)
    for span, value in update(1, before, latent_before_ref):
        advanced_ref[0, :, span] = jnp.where(first, entering_ref[:, span], value.astype(bf16))


def finish(level, first, returned, latent, latent_before, entering, gate_table):
    return pl.pallas_call(
        finish_kernel,
        out_shape=[jax.ShapeDtypeStruct(latent.shape, bf16)] * 2,
        in_specs=[SM] * 2 + [VM] * 5,
        out_specs=[VM] * 2,
        compiler_params=PARAMS,
    )(level, first, returned, latent, latent_before, entering, gate_table)


def local(
    queries, keys, values, latent, entering, noise_level, token_counts, block_mask, gate_table
):
    x = lax.axis_index("x")
    sources = [
        pltpu.with_memory_space_constraint(source, pltpu.HBM)
        for source in (queries, keys, values, latent)
    ]
    packed, latent_level = pack(noise_level, *sources)
    packed = lax.all_to_all(packed, HEAD_AXES, split_axis=0, concat_axis=0, tiled=True)
    packed, latent_level = lax.optimization_barrier((packed, latent_level))
    q, kv = unpack(packed)
    q = lax.all_gather(q, "x", axis=0, tiled=False)
    kv = lax.all_to_all(kv, "y", split_axis=0, concat_axis=0, tiled=True)
    kv = kv.reshape(4, 4, 8, 2, ROWS, HD)
    onward = [(s, s + 1) for s in range(15)]
    latent_before = lax.ppermute(latent_level, ("x", "zh"), onward)
    padded = jnp.concatenate([block_mask, jnp.zeros_like(block_mask)], axis=0)
    flags = lax.dynamic_slice(padded, (4 * x, 4 * x), (16, 4))
    counts = lax.dynamic_slice(token_counts, (4 * x,), (4,))
    place = x.reshape(1)
    last, part2, part3, k, v = attend_far(counts, flags, place, q, kv)
    part2, part3, latent_before = lax.optimization_barrier((part2, part3, latent_before))

    def onward_in_x(part, steps):
        return lax.ppermute(part, "x", [(source, source + steps) for source in range(4 - steps)])

    received3, received2 = onward_in_x(part3, 3), onward_in_x(part2, 2)
    own_last, own_rest, part1 = attend_next(flags, place, q, k, v, last)
    received1 = onward_in_x(part1, 1)
    q, received2, received3 = lax.optimization_barrier((q, received2, received3))
    own = attend_own(flags, place, q, k, v, own_rest)
    attended = merge(place, [own, own_last, received1, received2, received3])
    returned = lax.all_to_all(attended, HEAD_AXES, split_axis=0, concat_axis=0, tiled=True)
    first = ((x == 0) & (lax.axis_index("zh") == 0)).astype(jnp.int32).reshape(1)
    return tuple(
        finish(
            noise_level, first, returned, latent, latent_before, entering, gate_table
        )
    )


def solution(mesh):
    fine = Mesh(mesh.devices.reshape(4, 4, 4, 4, 2), ("x", "zh", "zl", "y", "c"))
    section, seq = ("x", "zh"), ("zl", "y", "c")
    placed = (
        P(section, seq, None),
        P(section, seq, None),
        P(section, seq, None),
        P(section, seq, None),
        P(seq, None),
        P(section),
        P(),
        P(),
        P(),
    )
    return jax.shard_map(
        local,
        mesh=fine,
        in_specs=placed,
        out_specs=(P(section, seq, None), P(section, seq, None)),
        check_vma=False,
    )
```

```python
import math

import jax
import jax.numpy as jnp
from jax import lax
from jax.experimental import pallas as pl
from jax.experimental.pallas import tpu as pltpu
from jax.sharding import Mesh
from jax.sharding import PartitionSpec as P

HD = 128
HEADS = 32
ROWS = 24
QUARTER = 192
BLOCK = 768
STAT = 16
SENT = 8
LANES = 256
SCALE = math.log2(math.e) / math.sqrt(HD)
LOW = -1e30
f32 = jnp.float32
bf16 = jnp.bfloat16

VM = pl.BlockSpec(memory_space=pltpu.VMEM)
SM = pl.BlockSpec(memory_space=pltpu.SMEM)
PARAMS = pltpu.CompilerParams(vmem_limit_bytes=48 * 2**20)
HEAD_AXES = ("zl", "zh", "c")
PAIR_ORDER = [(2 * (4 * zl + zh), 2 * (4 * zh + zl)) for zh in range(4) for zl in range(4)]


def pack_kernel(level_ref, q_hbm, k_hbm, v_hbm, latent_hbm, o_ref, latent_ref, buf, sems):
    sources = (q_hbm, k_hbm, v_hbm, latent_hbm)
    copies = [pltpu.make_async_copy(ref, buf.at[i], sems.at[i]) for i, ref in enumerate(sources)]
    for copy in copies:
        copy.start()
    latent_ref[0, :, HEADS * HD :] = jnp.full((ROWS, HD), level_ref[0], jnp.int32).astype(
        f32
    ).astype(bf16)
    for i in range(3):
        copies[i].wait()
        for h in range(HEADS):
            o_ref[h, i] = buf[i, 0, :, h * HD : (h + 1) * HD]
    copies[3].wait()
    latent_ref[0, :, : HEADS * HD] = buf[3, 0]


def pack(level, queries, keys, values, latent):
    hbm = pl.BlockSpec(memory_space=pltpu.HBM)
    return pl.pallas_call(
        pack_kernel,
        out_shape=[
            jax.ShapeDtypeStruct((HEADS, 3, ROWS, HD), bf16),
            jax.ShapeDtypeStruct((1, ROWS, HEADS * HD + HD), bf16),
        ],
        in_specs=[SM] + [hbm] * 4,
        out_specs=[VM] * 2,
        scratch_shapes=[
            pltpu.VMEM((4, 1, ROWS, HEADS * HD), bf16),
            pltpu.SemaphoreType.DMA((4,)),
        ],
        compiler_params=PARAMS,
    )(level, queries, keys, values, latent)


def unpack_kernel(packed_ref, q_ref, kv_ref):
    for source, place in PAIR_ORDER:
        q_ref[place : place + 2] = packed_ref[source : source + 2, 0]
        kv = packed_ref[source : source + 2, 1:]
        for copy in range(4):
            kv_ref[copy, place : place + 2] = kv


def unpack(packed):
    return pl.pallas_call(
        unpack_kernel,
        out_shape=[
            jax.ShapeDtypeStruct((HEADS, ROWS, HD), bf16),
            jax.ShapeDtypeStruct((4, HEADS, 2, ROWS, HD), bf16),
        ],
        in_specs=[VM],
        out_specs=[VM] * 2,
        compiler_params=PARAMS,
    )(packed)


def token_of(shape, dim):
    i = lax.broadcasted_iota(jnp.int32, shape, dim)
    one, nil = jnp.int32(1), jnp.int32(0)
    part = sum(jnp.where(i >= e * QUARTER, one, nil) for e in (1, 2, 3))
    inner = i - part * QUARTER
    run = sum(jnp.where(inner >= e * 48, one, nil) for e in (1, 2, 3))
    return inner + run * (QUARTER - 48) + part * 48


def list_units(units, flag_ref, slots, dummy):
    def build(e, n):
        slot, t = slots[0] + e // 4, e % 4
        active = flag_ref[slot * 4, t]
        for g in range(1, 4):
            active = active | flag_ref[slot * 4 + g, t]

        @pl.when(active == 1)
        def _():
            units[0, n] = slot
            units[1, n] = t

        return n + active

    n = lax.fori_loop(0, 4 * len(slots), build, jnp.int32(0))
    for i in range(2):
        units[0, n + i] = dummy
        units[1, n + i] = 0
    return n


def run_units(units, steps, flag_ref, q_sc, k_ref, v_ref, m_sc, acc_sc, s0, s1):
    real = q_sc.shape[0]
    lane = lax.broadcasted_iota(jnp.int32, (8, LANES), 1)

    def score(i, j, s):
        span = slice(j * LANES, (j + 1) * LANES)
        slot = jnp.minimum(units[0, i], real - 1)
        s[:, span] = lax.dot_general(
            k_ref[units[1, i]], q_sc[slot, span], (((1,), (1,)), ((), ())), preferred_element_type=f32
        )

    def weigh(i, j, s_read, s_write):
        span = slice(j * LANES, (j + 1) * LANES)
        slot, t = units[0, i], units[1, i]
        first = jnp.minimum(slot, real - 1) * 4
        flag = jnp.full((8, LANES), flag_ref[first + (j * LANES) // QUARTER, t], jnp.int32)
        for g in range(1, 4):
            if j * LANES < g * QUARTER < (j + 1) * LANES:
                flag = jnp.where(lane + j * LANES >= g * QUARTER, flag_ref[first + g, t], flag)
        on = flag == 1
        old = m_sc[slot, :, span]
        top = jnp.max(s_read[:, span], axis=0, keepdims=True) * SCALE
        new = jnp.where(on, jnp.maximum(old, top), old)
        m_sc[slot, :, span] = new
        a = jnp.exp2(old - new)
        p = jnp.exp2(s_read[:, span] * SCALE - jnp.where(on, new, -LOW)[:1]).astype(bf16)
        score(i + 1, j, s_write)
        part = jnp.dot(v_ref[t], p, preferred_element_type=f32)
        acc_sc[slot, :, span] = acc_sc[slot, :, span] * a[:1] + part

    def pair(h, carry):
        for j in steps:
            weigh(2 * h, j, s0, s1)
        for j in steps:
            weigh(2 * h + 1, j, s1, s0)
        return carry

    def run(n):
        for j in steps:
            score(0, j, s0)
        lax.fori_loop(0, (n + 1) // 2, pair, 0)

    return run


def clear(m_sc, acc_sc):
    m_sc[...] = jnp.full(m_sc.shape, LOW, f32)
    acc_sc[...] = jnp.zeros(acc_sc.shape, f32)


def partial(m, acc):
    total = acc[HD : HD + 1]
    some = total > 0.0
    safe = jnp.where(some, total, 1.0)
    level = jnp.where(some, m[:1] + jnp.log2(safe), LOW)
    hi = level.astype(bf16)
    mid = (level - hi.astype(f32)).astype(bf16)
    lo = (level - hi.astype(f32) - mid.astype(f32)).astype(bf16)
    stat = jnp.concatenate([hi, mid, lo, jnp.zeros((SENT - 3, level.shape[1]), bf16)], axis=0)
    return (acc[:HD] * (1.0 / safe)).astype(bf16), stat


def put(ref, span, part):
    head, stat = part
    ref[:HD, span] = head
    ref[HD:, span] = stat


def far_kernel(
    count_ref, flag_ref, place_ref, kv_ref, q_ref, o1_last, o2, o3, k_ref, v_ref,
    q_sc, m_sc, acc_sc, s0, s1, units,
):
    for slot in range(1, 4):
        q_sc[slot] = q_ref[jnp.minimum(place_ref[0] + slot, 3)].reshape(BLOCK, HD)

    token = token_of((BLOCK, HD), 0)
    token_row = token_of((STAT, BLOCK), 1)
    for t in range(4):
        k = jnp.concatenate([kv_ref[y, t, :, 0].reshape(QUARTER, HD) for y in range(4)])
        v = jnp.concatenate([kv_ref[y, t, :, 1].reshape(QUARTER, HD) for y in range(4)])
        valid = token < count_ref[t]
        k_ref[t] = jnp.where(valid, k, jnp.broadcast_to(k[0:1], k.shape))
        v_ref[t, :HD] = jnp.where(valid, v, jnp.zeros_like(v)).T
        v_ref[t, HD:] = jnp.where(token_row < count_ref[t], 1.0, 0.0).astype(bf16)

    clear(m_sc, acc_sc)
    refs = (flag_ref, q_sc, k_ref, v_ref, m_sc, acc_sc, s0, s1)
    run_units(units, (0, 1, 2), *refs)(list_units(units, flag_ref, (2, 3), 4))
    run_units(units, (2,), *refs)(list_units(units, flag_ref, (1,), 4))

    last = BLOCK - LANES
    part = partial(m_sc[1, :, last:], acc_sc[1, :, last:])
    put(o1_last, slice(0, LANES), part)
    for slot, ref in ((2, o2), (3, o3)):
        put(ref, slice(BLOCK, BLOCK + QUARTER), [piece[:, -QUARTER:] for piece in part])
        part = partial(m_sc[slot], acc_sc[slot])
        put(ref, slice(0, BLOCK), part)


def attend_rest(out_ref, units, flag_ref, q_sc, k_ref, v_ref, m_sc, acc_sc, s0, s1):
    dummy = q_sc.shape[0]
    refs = (flag_ref, q_sc, k_ref, v_ref, m_sc, acc_sc, s0, s1)
    run_units(units, (0, 1), *refs)(list_units(units, flag_ref, (0,), dummy))
    rest = BLOCK - LANES
    put(out_ref, slice(0, rest), partial(m_sc[0, :, :rest], acc_sc[0, :, :rest]))


def next_kernel(
    flag_ref, place_ref, q_ref, k_ref, v_ref, o1_last, o0_last, o0_rest, o1,
    q_sc, m_sc, acc_sc, s0, s1, units,
):
    for slot in range(2):
        q_sc[slot] = q_ref[jnp.minimum(place_ref[0] + slot, 3)].reshape(BLOCK, HD)
    clear(m_sc, acc_sc)
    refs = (flag_ref, q_sc, k_ref, v_ref, m_sc, acc_sc, s0, s1)
    run_units(units, (0, 1), *refs)(list_units(units, flag_ref, (1,), 2))
    run_units(units, (2,), *refs)(list_units(units, flag_ref, (0,), 2))
    last = BLOCK - LANES
    put(o1, slice(0, last), partial(m_sc[1, :, :last], acc_sc[1, :, :last]))
    o1[:, last:BLOCK] = o1_last[...]
    part = partial(m_sc[0, :, last:], acc_sc[0, :, last:])
    put(o0_last, slice(0, LANES), part)
    put(o1, slice(BLOCK, BLOCK + QUARTER), [piece[:, -QUARTER:] for piece in part])

    @pl.when(place_ref[0] >= 2)
    def _():
        attend_rest(o0_rest, units, *refs)

    @pl.when(place_ref[0] < 2)
    def _():
        o0_rest[...] = jnp.zeros(o0_rest.shape, bf16)


def own_kernel(
    flag_ref, place_ref, q_ref, k_ref, v_ref, rest_ref, o_ref, q_sc, m_sc, acc_sc, s0, s1, units
):
    @pl.when(place_ref[0] >= 2)
    def _():
        o_ref[...] = rest_ref[...]

    @pl.when(place_ref[0] < 2)
    def _():
        q_sc[0] = q_ref[place_ref[0]].reshape(BLOCK, HD)
        clear(m_sc, acc_sc)
        attend_rest(o_ref, units, flag_ref, q_sc, k_ref, v_ref, m_sc, acc_sc, s0, s1)


def scratch(slots):
    vmem = pltpu.VMEM
    return [
        vmem((slots, BLOCK, HD), bf16),
        vmem((slots + 1, 8, BLOCK), f32),
        vmem((slots + 1, HD + STAT, BLOCK), f32),
        vmem((BLOCK, BLOCK), f32),
        vmem((BLOCK, BLOCK), f32),
        pltpu.SMEM((2, 16), jnp.int32),
    ]


def cost(units):
    return pl.CostEstimate(
        flops=4 * units * BLOCK * BLOCK * HD,
        bytes_accessed=8 << 20,
        transcendentals=units * BLOCK * BLOCK,
    )


def result(columns):
    return jax.ShapeDtypeStruct((HD + SENT, columns), bf16)


def attend_far(counts, flags, place, q, kv):
    return pl.pallas_call(
        far_kernel,
        out_shape=[
            result(LANES),
            result(BLOCK + QUARTER),
            result(BLOCK + QUARTER),
            jax.ShapeDtypeStruct((4, BLOCK, HD), bf16),
            jax.ShapeDtypeStruct((4, HD + STAT, BLOCK), bf16),
        ],
        in_specs=[SM] * 3 + [VM] * 2,
        out_specs=[VM] * 5,
        scratch_shapes=scratch(4),
        compiler_params=PARAMS,
        cost_estimate=cost(10),
    )(counts, flags, place, kv, q)


def attend_next(flags, place, q, k, v, last):
    return pl.pallas_call(
        next_kernel,
        out_shape=[result(LANES), result(BLOCK - LANES), result(BLOCK + QUARTER)],
        in_specs=[SM] * 2 + [VM] * 4,
        out_specs=[VM] * 3,
        scratch_shapes=scratch(2),
        compiler_params=PARAMS,
        cost_estimate=cost(4),
    )(flags, place, q, k, v, last)


def attend_own(flags, place, q, k, v, rest):
    return pl.pallas_call(
        own_kernel,
        out_shape=result(BLOCK - LANES),
        in_specs=[SM] * 2 + [VM] * 4,
        out_specs=VM,
        scratch_shapes=scratch(1),
        compiler_params=PARAMS,
        cost_estimate=cost(4),
    )(flags, place, q, k, v, rest)


def blend(stats, heads):
    levels = [stat[0:1] + stat[1:2] + stat[2:3] for stat in stats]
    top = levels[0]
    for level in levels[1:]:
        top = jnp.maximum(top, level)
    shares = [jnp.exp2(level - top) for level in levels]
    whole = sum(shares[1:], shares[0])
    total = sum(head.astype(f32) * (share / whole) for head, share in zip(heads, shares))
    return total.astype(bf16).T


def merge_kernel(x_ref, r0, r0_last, r1, r2, r3, o_ref):
    own = jnp.concatenate([r0[...], r0_last[...]], axis=1)
    stats, heads = [own[HD:].astype(f32)], [own[:HD]]
    for k, ref in ((1, r1), (2, r2), (3, r3)):
        stat = ref[HD:].astype(f32)
        row = lax.broadcasted_iota(jnp.int32, stat.shape, 0)
        stats.append(jnp.where(x_ref[0] >= k, stat, jnp.where(row == 0, LOW, 0.0)))
        heads.append(ref[:HD])
    own = blend([stat[:, :BLOCK] for stat in stats], [head[:, :BLOCK] for head in heads])
    tail = blend([stat[:, BLOCK:] for stat in stats[1:]], [head[:, BLOCK:] for head in heads[1:]])
    own = own.reshape(HEADS, ROWS, HD)
    before = jnp.concatenate([tail.reshape(8, ROWS, HD), own[: HEADS - 8]])
    for target, place in PAIR_ORDER:
        o_ref[target : target + 2, 0] = own[place : place + 2]
        o_ref[target : target + 2, 1] = before[place : place + 2]


def merge(x, parts):
    return pl.pallas_call(
        merge_kernel,
        out_shape=jax.ShapeDtypeStruct((HEADS, 2, ROWS, HD), bf16),
        in_specs=[SM] + [VM] * 5,
        out_specs=VM,
        compiler_params=PARAMS,
    )(x, *parts)


def finish_kernel(
    level_ref, first_ref, r_ref, latent_ref, latent_before_ref, entering_ref, gate_ref,
    updated_ref, advanced_ref,
):
    def update(which, level, residual):
        squares = jnp.zeros((ROWS, HD), f32)
        for h in range(HEADS):
            wide = r_ref[h, which].astype(f32)
            squares = squares + wide * wide
        mean = jnp.sum(squares, axis=-1, keepdims=True) * (1.0 / (HEADS * HD))
        factor = 1.0 / jnp.sqrt(mean + 1e-06)
        index = lax.broadcasted_iota(jnp.int32, (gate_ref.shape[0], HD), 0)
        mine = index.astype(f32) == level
        for h in range(HEADS):
            span = slice(h * HD, (h + 1) * HD)
            gate = jnp.sum(jnp.where(mine, gate_ref[:, span], 0.0), axis=0, keepdims=True)
            wide = r_ref[h, which].astype(f32)
            yield span, residual[0, :, span].astype(f32) + gate * (wide * factor)

    for span, value in update(0, level_ref[0].astype(f32), latent_ref):
        updated_ref[0, :, span] = value.astype(bf16)
    first = first_ref[0] == 1
    before = latent_before_ref[0, :1, HEADS * HD :].astype(f32)
    for span, value in update(1, before, latent_before_ref):
        advanced_ref[0, :, span] = jnp.where(first, entering_ref[:, span], value.astype(bf16))


def finish(level, first, returned, latent, latent_before, entering, gate_table):
    return pl.pallas_call(
        finish_kernel,
        out_shape=[jax.ShapeDtypeStruct(latent.shape, bf16)] * 2,
        in_specs=[SM] * 2 + [VM] * 5,
        out_specs=[VM] * 2,
        compiler_params=PARAMS,
    )(level, first, returned, latent, latent_before, entering, gate_table)


def local(
    queries, keys, values, latent, entering, noise_level, token_counts, block_mask, gate_table
):
    x = lax.axis_index("x")
    sources = [
        pltpu.with_memory_space_constraint(source, pltpu.HBM)
        for source in (queries, keys, values, latent)
    ]
    packed, latent_level = pack(noise_level, *sources)
    packed = lax.all_to_all(packed, HEAD_AXES, split_axis=0, concat_axis=0, tiled=True)
    packed, latent_level = lax.optimization_barrier((packed, latent_level))
    q, kv = unpack(packed)
    q = lax.all_gather(q, "x", axis=0, tiled=False)
    kv = lax.all_to_all(kv, "y", split_axis=0, concat_axis=0, tiled=True)
    kv = kv.reshape(4, 4, 8, 2, ROWS, HD)
    onward = [(s, s + 1) for s in range(15)]
    latent_before = lax.ppermute(latent_level, ("x", "zh"), onward)
    padded = jnp.concatenate([block_mask, jnp.zeros_like(block_mask)], axis=0)
    flags = lax.dynamic_slice(padded, (4 * x, 4 * x), (16, 4))
    counts = lax.dynamic_slice(token_counts, (4 * x,), (4,))
    place = x.reshape(1)
    last, part2, part3, k, v = attend_far(counts, flags, place, q, kv)
    part2, part3, latent_before = lax.optimization_barrier((part2, part3, latent_before))

    def onward_in_x(part, steps):
        return lax.ppermute(part, "x", [(source, source + steps) for source in range(4 - steps)])

    received3, received2 = onward_in_x(part3, 3), onward_in_x(part2, 2)
    own_last, own_rest, part1 = attend_next(flags, place, q, k, v, last)
    received1 = onward_in_x(part1, 1)
    q, received2, received3 = lax.optimization_barrier((q, received2, received3))
    own = attend_own(flags, place, q, k, v, own_rest)
    attended = merge(place, [own, own_last, received1, received2, received3])
    returned = lax.all_to_all(attended, HEAD_AXES, split_axis=0, concat_axis=0, tiled=True)
    first = ((x == 0) & (lax.axis_index("zh") == 0)).astype(jnp.int32).reshape(1)
    return tuple(
        finish(
            noise_level, first, returned, latent, latent_before, entering, gate_table
        )
    )


def solution(mesh):
    fine = Mesh(mesh.devices.reshape(4, 4, 4, 4, 2), ("x", "zh", "zl", "y", "c"))
    section, seq = ("x", "zh"), ("zl", "y", "c")
    placed = (
        P(section, seq, None),
        P(section, seq, None),
        P(section, seq, None),
        P(section, seq, None),
        P(seq, None),
        P(section),
        P(),
        P(),
        P(),
    )
    return jax.shard_map(
        local,
        mesh=fine,
        in_specs=placed,
        out_specs=(P(section, seq, None), P(section, seq, None)),
        check_vma=False,
    )
```

```python
import math

import jax
import jax.numpy as jnp
from jax import lax
from jax.experimental import pallas as pl
from jax.experimental.pallas import tpu as pltpu
from jax.sharding import Mesh
from jax.sharding import PartitionSpec as P

HD = 128
HEADS = 32
ROWS = 24
QUARTER = 192
BLOCK = 768
STAT = 16
SENT = 8
LANES = 256
SCALE = math.log2(math.e) / math.sqrt(HD)
LOW = -1e30
f32 = jnp.float32
bf16 = jnp.bfloat16

VM = pl.BlockSpec(memory_space=pltpu.VMEM)
SM = pl.BlockSpec(memory_space=pltpu.SMEM)
PARAMS = pltpu.CompilerParams(vmem_limit_bytes=48 * 2**20)
HEAD_AXES = ("zl", "zh", "c")
PAIR_ORDER = [(2 * (4 * zl + zh), 2 * (4 * zh + zl)) for zh in range(4) for zl in range(4)]


def pack_kernel(level_ref, q_hbm, k_hbm, v_hbm, latent_hbm, o_ref, latent_ref, buf, sems):
    sources = (q_hbm, k_hbm, v_hbm, latent_hbm)
    copies = [pltpu.make_async_copy(ref, buf.at[i], sems.at[i]) for i, ref in enumerate(sources)]
    for copy in copies:
        copy.start()
    latent_ref[0, :, HEADS * HD :] = jnp.full((ROWS, HD), level_ref[0], jnp.int32).astype(
        f32
    ).astype(bf16)
    for i in range(3):
        copies[i].wait()
        for h in range(HEADS):
            o_ref[h, i] = buf[i, 0, :, h * HD : (h + 1) * HD]
    copies[3].wait()
    latent_ref[0, :, : HEADS * HD] = buf[3, 0]


def pack(level, queries, keys, values, latent):
    hbm = pl.BlockSpec(memory_space=pltpu.HBM)
    return pl.pallas_call(
        pack_kernel,
        out_shape=[
            jax.ShapeDtypeStruct((HEADS, 3, ROWS, HD), bf16),
            jax.ShapeDtypeStruct((1, ROWS, HEADS * HD + HD), bf16),
        ],
        in_specs=[SM] + [hbm] * 4,
        out_specs=[VM] * 2,
        scratch_shapes=[
            pltpu.VMEM((4, 1, ROWS, HEADS * HD), bf16),
            pltpu.SemaphoreType.DMA((4,)),
        ],
        compiler_params=PARAMS,
    )(level, queries, keys, values, latent)


def unpack_kernel(packed_ref, q_ref, kv_ref):
    for source, place in PAIR_ORDER:
        q_ref[place : place + 2] = packed_ref[source : source + 2, 0]
        kv = packed_ref[source : source + 2, 1:]
        for copy in range(4):
            kv_ref[copy, place : place + 2] = kv


def unpack(packed):
    return pl.pallas_call(
        unpack_kernel,
        out_shape=[
            jax.ShapeDtypeStruct((HEADS, ROWS, HD), bf16),
            jax.ShapeDtypeStruct((4, HEADS, 2, ROWS, HD), bf16),
        ],
        in_specs=[VM],
        out_specs=[VM] * 2,
        compiler_params=PARAMS,
    )(packed)


def token_of(shape, dim):
    i = lax.broadcasted_iota(jnp.int32, shape, dim)
    one, nil = jnp.int32(1), jnp.int32(0)
    part = sum(jnp.where(i >= e * QUARTER, one, nil) for e in (1, 2, 3))
    inner = i - part * QUARTER
    run = sum(jnp.where(inner >= e * 48, one, nil) for e in (1, 2, 3))
    return inner + run * (QUARTER - 48) + part * 48


def list_units(units, flag_ref, slots, dummy):
    def build(e, n):
        slot, t = slots[0] + e // 4, e % 4
        active = flag_ref[slot * 4, t]
        for g in range(1, 4):
            active = active | flag_ref[slot * 4 + g, t]

        @pl.when(active == 1)
        def _():
            units[0, n] = slot
            units[1, n] = t

        return n + active

    n = lax.fori_loop(0, 4 * len(slots), build, jnp.int32(0))
    for i in range(2):
        units[0, n + i] = dummy
        units[1, n + i] = 0
    return n


def run_units(units, steps, flag_ref, q_sc, k_ref, v_ref, m_sc, acc_sc, s0, s1):
    real = q_sc.shape[0]
    lane = lax.broadcasted_iota(jnp.int32, (8, LANES), 1)

    def score(i, j, s):
        span = slice(j * LANES, (j + 1) * LANES)
        slot = jnp.minimum(units[0, i], real - 1)
        s[:, span] = lax.dot_general(
            k_ref[units[1, i]], q_sc[slot, span], (((1,), (1,)), ((), ())), preferred_element_type=f32
        )

    def weigh(i, j, s_read, s_write):
        span = slice(j * LANES, (j + 1) * LANES)
        slot, t = units[0, i], units[1, i]
        first = jnp.minimum(slot, real - 1) * 4
        flag = jnp.full((8, LANES), flag_ref[first + (j * LANES) // QUARTER, t], jnp.int32)
        for g in range(1, 4):
            if j * LANES < g * QUARTER < (j + 1) * LANES:
                flag = jnp.where(lane + j * LANES >= g * QUARTER, flag_ref[first + g, t], flag)
        on = flag == 1
        old = m_sc[slot, :, span]
        top = jnp.max(s_read[:, span], axis=0, keepdims=True) * SCALE
        new = jnp.where(on, jnp.maximum(old, top), old)
        m_sc[slot, :, span] = new
        a = jnp.exp2(old - new)
        p = jnp.exp2(s_read[:, span] * SCALE - jnp.where(on, new, -LOW)[:1]).astype(bf16)
        score(i + 1, j, s_write)
        part = jnp.dot(v_ref[t], p, preferred_element_type=f32)
        acc_sc[slot, :, span] = acc_sc[slot, :, span] * a[:1] + part

    def pair(h, carry):
        for j in steps:
            weigh(2 * h, j, s0, s1)
        for j in steps:
            weigh(2 * h + 1, j, s1, s0)
        return carry

    def run(n):
        for j in steps:
            score(0, j, s0)
        lax.fori_loop(0, (n + 1) // 2, pair, 0)

    return run


def clear(m_sc, acc_sc):
    m_sc[...] = jnp.full(m_sc.shape, LOW, f32)
    acc_sc[...] = jnp.zeros(acc_sc.shape, f32)


def partial(m, acc):
    total = acc[HD : HD + 1]
    some = total > 0.0
    safe = jnp.where(some, total, 1.0)
    level = jnp.where(some, m[:1] + jnp.log2(safe), LOW)
    hi = level.astype(bf16)
    mid = (level - hi.astype(f32)).astype(bf16)
    lo = (level - hi.astype(f32) - mid.astype(f32)).astype(bf16)
    stat = jnp.concatenate([hi, mid, lo, jnp.zeros((SENT - 3, level.shape[1]), bf16)], axis=0)
    return (acc[:HD] * (1.0 / safe)).astype(bf16), stat


def put(ref, span, part):
    head, stat = part
    ref[:HD, span] = head
    ref[HD:, span] = stat


def far_kernel(
    count_ref, flag_ref, kv_ref, q1_ref, q2_ref, q3_ref, o1_last, o2, o3, k_ref, v_ref,
    q_sc, m_sc, acc_sc, s0, s1, units,
):
    for slot, ref in ((1, q1_ref), (2, q2_ref), (3, q3_ref)):
        q_sc[slot] = ref[...].reshape(BLOCK, HD)

    token = token_of((BLOCK, HD), 0)
    token_row = token_of((STAT, BLOCK), 1)
    for t in range(4):
        k = jnp.concatenate([kv_ref[y, t, :, 0].reshape(QUARTER, HD) for y in range(4)])
        v = jnp.concatenate([kv_ref[y, t, :, 1].reshape(QUARTER, HD) for y in range(4)])
        valid = token < count_ref[t]
        k_ref[t] = jnp.where(valid, k, jnp.broadcast_to(k[0:1], k.shape))
        v_ref[t, :HD] = jnp.where(valid, v, jnp.zeros_like(v)).T
        v_ref[t, HD:] = jnp.where(token_row < count_ref[t], 1.0, 0.0).astype(bf16)

    clear(m_sc, acc_sc)
    refs = (flag_ref, q_sc, k_ref, v_ref, m_sc, acc_sc, s0, s1)
    run_units(units, (0, 1, 2), *refs)(list_units(units, flag_ref, (2, 3), 4))
    run_units(units, (2,), *refs)(list_units(units, flag_ref, (1,), 4))

    last = BLOCK - LANES
    part = partial(m_sc[1, :, last:], acc_sc[1, :, last:])
    put(o1_last, slice(0, LANES), part)
    for slot, ref in ((2, o2), (3, o3)):
        put(ref, slice(BLOCK, BLOCK + QUARTER), [piece[:, -QUARTER:] for piece in part])
        part = partial(m_sc[slot], acc_sc[slot])
        put(ref, slice(0, BLOCK), part)


def attend_rest(out_ref, units, flag_ref, q_sc, k_ref, v_ref, m_sc, acc_sc, s0, s1):
    dummy = q_sc.shape[0]
    refs = (flag_ref, q_sc, k_ref, v_ref, m_sc, acc_sc, s0, s1)
    run_units(units, (0, 1), *refs)(list_units(units, flag_ref, (0,), dummy))
    rest = BLOCK - LANES
    put(out_ref, slice(0, rest), partial(m_sc[0, :, :rest], acc_sc[0, :, :rest]))


def next_kernel(
    flag_ref, place_ref, q0_ref, q1_ref, k_ref, v_ref, o1_last, o0_last, o0_rest, o1,
    q_sc, m_sc, acc_sc, s0, s1, units,
):
    for slot, ref in ((0, q0_ref), (1, q1_ref)):
        q_sc[slot] = ref[...].reshape(BLOCK, HD)
    clear(m_sc, acc_sc)
    refs = (flag_ref, q_sc, k_ref, v_ref, m_sc, acc_sc, s0, s1)
    run_units(units, (0, 1), *refs)(list_units(units, flag_ref, (1,), 2))
    run_units(units, (2,), *refs)(list_units(units, flag_ref, (0,), 2))
    last = BLOCK - LANES
    put(o1, slice(0, last), partial(m_sc[1, :, :last], acc_sc[1, :, :last]))
    o1[:, last:BLOCK] = o1_last[...]
    part = partial(m_sc[0, :, last:], acc_sc[0, :, last:])
    put(o0_last, slice(0, LANES), part)
    put(o1, slice(BLOCK, BLOCK + QUARTER), [piece[:, -QUARTER:] for piece in part])

    @pl.when(place_ref[0] >= 2)
    def _():
        attend_rest(o0_rest, units, *refs)

    @pl.when(place_ref[0] < 2)
    def _():
        o0_rest[...] = jnp.zeros(o0_rest.shape, bf16)


def own_kernel(
    flag_ref, place_ref, q_ref, k_ref, v_ref, rest_ref, o_ref, q_sc, m_sc, acc_sc, s0, s1, units
):
    @pl.when(place_ref[0] >= 2)
    def _():
        o_ref[...] = rest_ref[...]

    @pl.when(place_ref[0] < 2)
    def _():
        q_sc[0] = q_ref[...].reshape(BLOCK, HD)
        clear(m_sc, acc_sc)
        attend_rest(o_ref, units, flag_ref, q_sc, k_ref, v_ref, m_sc, acc_sc, s0, s1)


def scratch(slots):
    vmem = pltpu.VMEM
    return [
        vmem((slots, BLOCK, HD), bf16),
        vmem((slots + 1, 8, BLOCK), f32),
        vmem((slots + 1, HD + STAT, BLOCK), f32),
        vmem((BLOCK, BLOCK), f32),
        vmem((BLOCK, BLOCK), f32),
        pltpu.SMEM((2, 16), jnp.int32),
    ]


def cost(units):
    return pl.CostEstimate(
        flops=4 * units * BLOCK * BLOCK * HD,
        bytes_accessed=8 << 20,
        transcendentals=units * BLOCK * BLOCK,
    )


def result(columns):
    return jax.ShapeDtypeStruct((HD + SENT, columns), bf16)


def attend_far(counts, flags, kv, q1, q2, q3):
    return pl.pallas_call(
        far_kernel,
        out_shape=[
            result(LANES),
            result(BLOCK + QUARTER),
            result(BLOCK + QUARTER),
            jax.ShapeDtypeStruct((4, BLOCK, HD), bf16),
            jax.ShapeDtypeStruct((4, HD + STAT, BLOCK), bf16),
        ],
        in_specs=[SM] * 2 + [VM] * 4,
        out_specs=[VM] * 5,
        scratch_shapes=scratch(4),
        compiler_params=PARAMS,
        cost_estimate=cost(10),
    )(counts, flags, kv, q1, q2, q3)


def attend_next(flags, place, q0, q1, k, v, last):
    return pl.pallas_call(
        next_kernel,
        out_shape=[result(LANES), result(BLOCK - LANES), result(BLOCK + QUARTER)],
        in_specs=[SM] * 2 + [VM] * 5,
        out_specs=[VM] * 3,
        scratch_shapes=scratch(2),
        compiler_params=PARAMS,
        cost_estimate=cost(4),
    )(flags, place, q0, q1, k, v, last)


def attend_own(flags, place, q, k, v, rest):
    return pl.pallas_call(
        own_kernel,
        out_shape=result(BLOCK - LANES),
        in_specs=[SM] * 2 + [VM] * 4,
        out_specs=VM,
        scratch_shapes=scratch(1),
        compiler_params=PARAMS,
        cost_estimate=cost(4),
    )(flags, place, q, k, v, rest)


def blend(stats, heads):
    levels = [stat[0:1] + stat[1:2] + stat[2:3] for stat in stats]
    top = levels[0]
    for level in levels[1:]:
        top = jnp.maximum(top, level)
    shares = [jnp.exp2(level - top) for level in levels]
    whole = sum(shares[1:], shares[0])
    total = sum(head.astype(f32) * (share / whole) for head, share in zip(heads, shares))
    return total.astype(bf16).T


def merge_kernel(x_ref, r0, r0_last, r1, r2, r3, o_ref):
    own = jnp.concatenate([r0[...], r0_last[...]], axis=1)
    stats, heads = [own[HD:].astype(f32)], [own[:HD]]
    for k, ref in ((1, r1), (2, r2), (3, r3)):
        stat = ref[HD:].astype(f32)
        row = lax.broadcasted_iota(jnp.int32, stat.shape, 0)
        stats.append(jnp.where(x_ref[0] >= k, stat, jnp.where(row == 0, LOW, 0.0)))
        heads.append(ref[:HD])
    own = blend([stat[:, :BLOCK] for stat in stats], [head[:, :BLOCK] for head in heads])
    tail = blend([stat[:, BLOCK:] for stat in stats[1:]], [head[:, BLOCK:] for head in heads[1:]])
    own = own.reshape(HEADS, ROWS, HD)
    before = jnp.concatenate([tail.reshape(8, ROWS, HD), own[: HEADS - 8]])
    for target, place in PAIR_ORDER:
        o_ref[target : target + 2, 0] = own[place : place + 2]
        o_ref[target : target + 2, 1] = before[place : place + 2]


def merge(x, parts):
    return pl.pallas_call(
        merge_kernel,
        out_shape=jax.ShapeDtypeStruct((HEADS, 2, ROWS, HD), bf16),
        in_specs=[SM] + [VM] * 5,
        out_specs=VM,
        compiler_params=PARAMS,
    )(x, *parts)


def finish_kernel(
    level_ref, first_ref, r_ref, latent_ref, latent_before_ref, entering_ref, gate_ref,
    updated_ref, advanced_ref,
):
    def update(which, level, residual):
        squares = jnp.zeros((ROWS, HD), f32)
        for h in range(HEADS):
            wide = r_ref[h, which].astype(f32)
            squares = squares + wide * wide
        mean = jnp.sum(squares, axis=-1, keepdims=True) * (1.0 / (HEADS * HD))
        factor = 1.0 / jnp.sqrt(mean + 1e-06)
        index = lax.broadcasted_iota(jnp.int32, (gate_ref.shape[0], HD), 0)
        mine = index.astype(f32) == level
        for h in range(HEADS):
            span = slice(h * HD, (h + 1) * HD)
            gate = jnp.sum(jnp.where(mine, gate_ref[:, span], 0.0), axis=0, keepdims=True)
            wide = r_ref[h, which].astype(f32)
            yield span, residual[0, :, span].astype(f32) + gate * (wide * factor)

    for span, value in update(0, level_ref[0].astype(f32), latent_ref):
        updated_ref[0, :, span] = value.astype(bf16)
    first = first_ref[0] == 1
    before = latent_before_ref[0, :1, HEADS * HD :].astype(f32)
    for span, value in update(1, before, latent_before_ref):
        advanced_ref[0, :, span] = jnp.where(first, entering_ref[:, span], value.astype(bf16))


def finish(level, first, returned, latent, latent_before, entering, gate_table):
    return pl.pallas_call(
        finish_kernel,
        out_shape=[jax.ShapeDtypeStruct(latent.shape, bf16)] * 2,
        in_specs=[SM] * 2 + [VM] * 5,
        out_specs=[VM] * 2,
        compiler_params=PARAMS,
    )(level, first, returned, latent, latent_before, entering, gate_table)


def local(
    queries, keys, values, latent, entering, noise_level, token_counts, block_mask, gate_table
):
    x = lax.axis_index("x")
    sources = [
        pltpu.with_memory_space_constraint(source, pltpu.HBM)
        for source in (queries, keys, values, latent)
    ]
    packed, latent_level = pack(noise_level, *sources)
    packed = lax.all_to_all(packed, HEAD_AXES, split_axis=0, concat_axis=0, tiled=True)
    packed, latent_level = lax.optimization_barrier((packed, latent_level))
    q, kv = unpack(packed)
    q1, q2, q3 = (
        lax.ppermute(q, "x", [(source, source - steps) for source in range(steps, 4)])
        for steps in (1, 2, 3)
    )
    kv = lax.all_to_all(kv, "y", split_axis=0, concat_axis=0, tiled=True)
    kv = kv.reshape(4, 4, 8, 2, ROWS, HD)
    onward = [(s, s + 1) for s in range(15)]
    latent_before = lax.ppermute(latent_level, ("x", "zh"), onward)
    padded = jnp.concatenate([block_mask, jnp.zeros_like(block_mask)], axis=0)
    flags = lax.dynamic_slice(padded, (4 * x, 4 * x), (16, 4))
    counts = lax.dynamic_slice(token_counts, (4 * x,), (4,))
    place = x.reshape(1)
    last, part2, part3, k, v = attend_far(counts, flags, kv, q1, q2, q3)

    def onward_in_x(part, steps):
        return lax.ppermute(part, "x", [(source, source + steps) for source in range(4 - steps)])

    received3, received2 = onward_in_x(part3, 3), onward_in_x(part2, 2)
    own_last, own_rest, part1 = attend_next(flags, place, q, q1, k, v, last)
    received1 = onward_in_x(part1, 1)
    q, received2, received3, latent_before = lax.optimization_barrier(
        (q, received2, received3, latent_before)
    )
    own = attend_own(flags, place, q, k, v, own_rest)
    attended = merge(place, [own, own_last, received1, received2, received3])
    returned = lax.all_to_all(attended, HEAD_AXES, split_axis=0, concat_axis=0, tiled=True)
    first = ((x == 0) & (lax.axis_index("zh") == 0)).astype(jnp.int32).reshape(1)
    return tuple(
        finish(
            noise_level, first, returned, latent, latent_before, entering, gate_table
        )
    )


def solution(mesh):
    fine = Mesh(mesh.devices.reshape(4, 4, 4, 4, 2), ("x", "zh", "zl", "y", "c"))
    section, seq = ("x", "zh"), ("zl", "y", "c")
    placed = (
        P(section, seq, None),
        P(section, seq, None),
        P(section, seq, None),
        P(section, seq, None),
        P(seq, None),
        P(section),
        P(),
        P(),
        P(),
    )
    return jax.shard_map(
        local,
        mesh=fine,
        in_specs=placed,
        out_specs=(P(section, seq, None), P(section, seq, None)),
        check_vma=False,
    )
```

```python
import math

import jax
import jax.numpy as jnp
from jax import lax
from jax.experimental import pallas as pl
from jax.experimental.pallas import tpu as pltpu
from jax.sharding import Mesh
from jax.sharding import PartitionSpec as P

HD = 128
HEADS = 32
ROWS = 24
QUARTER = 192
BLOCK = 768
STAT = 16
SENT = 8
LANES = 256
SCALE = math.log2(math.e) / math.sqrt(HD)
LOW = -1e30
f32 = jnp.float32
bf16 = jnp.bfloat16

VM = pl.BlockSpec(memory_space=pltpu.VMEM)
SM = pl.BlockSpec(memory_space=pltpu.SMEM)
PARAMS = pltpu.CompilerParams(vmem_limit_bytes=48 * 2**20)
HEAD_AXES = ("zl", "zh", "c")
PAIR_ORDER = [(2 * (4 * zl + zh), 2 * (4 * zh + zl)) for zh in range(4) for zl in range(4)]


def pack_kernel(level_ref, q_hbm, k_hbm, v_hbm, latent_hbm, o_ref, latent_ref, buf, sems):
    sources = (q_hbm, k_hbm, v_hbm, latent_hbm)
    copies = [pltpu.make_async_copy(ref, buf.at[i], sems.at[i]) for i, ref in enumerate(sources)]
    for copy in copies:
        copy.start()
    latent_ref[0, :, HEADS * HD :] = jnp.full((ROWS, HD), level_ref[0], jnp.int32).astype(
        f32
    ).astype(bf16)
    for i in range(3):
        copies[i].wait()
        for h in range(HEADS):
            o_ref[h, i] = buf[i, 0, :, h * HD : (h + 1) * HD]
    copies[3].wait()
    latent_ref[0, :, : HEADS * HD] = buf[3, 0]


def pack(level, queries, keys, values, latent):
    hbm = pl.BlockSpec(memory_space=pltpu.HBM)
    return pl.pallas_call(
        pack_kernel,
        out_shape=[
            jax.ShapeDtypeStruct((HEADS, 3, ROWS, HD), bf16),
            jax.ShapeDtypeStruct((1, ROWS, HEADS * HD + HD), bf16),
        ],
        in_specs=[SM] + [hbm] * 4,
        out_specs=[VM] * 2,
        scratch_shapes=[
            pltpu.VMEM((4, 1, ROWS, HEADS * HD), bf16),
            pltpu.SemaphoreType.DMA((4,)),
        ],
        compiler_params=PARAMS,
    )(level, queries, keys, values, latent)


def unpack_kernel(packed_ref, q_ref, kv_ref):
    for source, place in PAIR_ORDER:
        q_ref[place : place + 2] = packed_ref[source : source + 2, 0]
        kv = packed_ref[source : source + 2, 1:]
        for copy in range(4):
            kv_ref[copy, place : place + 2] = kv


def unpack(packed):
    return pl.pallas_call(
        unpack_kernel,
        out_shape=[
            jax.ShapeDtypeStruct((HEADS, ROWS, HD), bf16),
            jax.ShapeDtypeStruct((4, HEADS, 2, ROWS, HD), bf16),
        ],
        in_specs=[VM],
        out_specs=[VM] * 2,
        compiler_params=PARAMS,
    )(packed)


def token_of(shape, dim):
    i = lax.broadcasted_iota(jnp.int32, shape, dim)
    one, nil = jnp.int32(1), jnp.int32(0)
    part = sum(jnp.where(i >= e * QUARTER, one, nil) for e in (1, 2, 3))
    inner = i - part * QUARTER
    run = sum(jnp.where(inner >= e * 48, one, nil) for e in (1, 2, 3))
    return inner + run * (QUARTER - 48) + part * 48


def list_units(units, flag_ref, slots, dummy):
    def build(e, n):
        slot, t = slots[0] + e // 4, e % 4
        active = flag_ref[slot * 4, t]
        for g in range(1, 4):
            active = active | flag_ref[slot * 4 + g, t]

        @pl.when(active == 1)
        def _():
            units[0, n] = slot
            units[1, n] = t

        return n + active

    n = lax.fori_loop(0, 4 * len(slots), build, jnp.int32(0))
    for i in range(2):
        units[0, n + i] = dummy
        units[1, n + i] = 0
    return n


def run_units(units, steps, flag_ref, q_sc, k_ref, v_ref, m_sc, acc_sc, s0, s1):
    real = q_sc.shape[0]
    lane = lax.broadcasted_iota(jnp.int32, (8, LANES), 1)

    def score(i, j, s):
        span = slice(j * LANES, (j + 1) * LANES)
        slot = jnp.minimum(units[0, i], real - 1)
        s[:, span] = lax.dot_general(
            k_ref[units[1, i]], q_sc[slot, span], (((1,), (1,)), ((), ())), preferred_element_type=f32
        )

    def weigh(i, j, s_read, s_write):
        span = slice(j * LANES, (j + 1) * LANES)
        slot, t = units[0, i], units[1, i]
        first = jnp.minimum(slot, real - 1) * 4
        flag = jnp.full((8, LANES), flag_ref[first + (j * LANES) // QUARTER, t], jnp.int32)
        for g in range(1, 4):
            if j * LANES < g * QUARTER < (j + 1) * LANES:
                flag = jnp.where(lane + j * LANES >= g * QUARTER, flag_ref[first + g, t], flag)
        on = flag == 1
        old = m_sc[slot, :, span]
        top = jnp.max(s_read[:, span], axis=0, keepdims=True) * SCALE
        new = jnp.where(on, jnp.maximum(old, top), old)
        m_sc[slot, :, span] = new
        a = jnp.exp2(old - new)
        p = jnp.exp2(s_read[:, span] * SCALE - jnp.where(on, new, -LOW)[:1]).astype(bf16)
        score(i + 1, j, s_write)
        part = jnp.dot(v_ref[t], p, preferred_element_type=f32)
        acc_sc[slot, :, span] = acc_sc[slot, :, span] * a[:1] + part

    def pair(h, carry):
        for j in steps:
            weigh(2 * h, j, s0, s1)
        for j in steps:
            weigh(2 * h + 1, j, s1, s0)
        return carry

    def run(n):
        for j in steps:
            score(0, j, s0)
        lax.fori_loop(0, (n + 1) // 2, pair, 0)

    return run


def clear(m_sc, acc_sc):
    m_sc[...] = jnp.full(m_sc.shape, LOW, f32)
    acc_sc[...] = jnp.zeros(acc_sc.shape, f32)


def partial(m, acc):
    total = acc[HD : HD + 1]
    some = total > 0.0
    safe = jnp.where(some, total, 1.0)
    level = jnp.where(some, m[:1] + jnp.log2(safe), LOW)
    hi = level.astype(bf16)
    mid = (level - hi.astype(f32)).astype(bf16)
    lo = (level - hi.astype(f32) - mid.astype(f32)).astype(bf16)
    stat = jnp.concatenate([hi, mid, lo, jnp.zeros((SENT - 3, level.shape[1]), bf16)], axis=0)
    return (acc[:HD] * (1.0 / safe)).astype(bf16), stat


def put(ref, span, part):
    head, stat = part
    ref[:HD, span] = head
    ref[HD:, span] = stat


def far_kernel(
    count_ref, flag_ref, kv_ref, q1_ref, q2_ref, q3_ref, o1_last, o2, o3, k_ref, v_ref,
    q_sc, m_sc, acc_sc, s0, s1, units,
):
    for slot, ref in ((1, q1_ref), (2, q2_ref), (3, q3_ref)):
        q_sc[slot] = ref[...].reshape(BLOCK, HD)

    token = token_of((BLOCK, HD), 0)
    token_row = token_of((STAT, BLOCK), 1)
    for t in range(4):
        k = jnp.concatenate([kv_ref[y, t, :, 0].reshape(QUARTER, HD) for y in range(4)])
        v = jnp.concatenate([kv_ref[y, t, :, 1].reshape(QUARTER, HD) for y in range(4)])
        valid = token < count_ref[t]
        k_ref[t] = jnp.where(valid, k, jnp.broadcast_to(k[0:1], k.shape))
        v_ref[t, :HD] = jnp.where(valid, v, jnp.zeros_like(v)).T
        v_ref[t, HD:] = jnp.where(token_row < count_ref[t], 1.0, 0.0).astype(bf16)

    clear(m_sc, acc_sc)
    refs = (flag_ref, q_sc, k_ref, v_ref, m_sc, acc_sc, s0, s1)
    run_units(units, (0, 1, 2), *refs)(list_units(units, flag_ref, (2, 3), 4))
    run_units(units, (2,), *refs)(list_units(units, flag_ref, (1,), 4))

    last = BLOCK - LANES
    part = partial(m_sc[1, :, last:], acc_sc[1, :, last:])
    put(o1_last, slice(0, LANES), part)
    for slot, ref in ((2, o2), (3, o3)):
        put(ref, slice(BLOCK, BLOCK + QUARTER), [piece[:, -QUARTER:] for piece in part])
        part = partial(m_sc[slot], acc_sc[slot])
        put(ref, slice(0, BLOCK), part)


def attend_rest(out_ref, units, flag_ref, q_sc, k_ref, v_ref, m_sc, acc_sc, s0, s1):
    dummy = q_sc.shape[0]
    refs = (flag_ref, q_sc, k_ref, v_ref, m_sc, acc_sc, s0, s1)
    run_units(units, (0, 1), *refs)(list_units(units, flag_ref, (0,), dummy))
    rest = BLOCK - LANES
    put(out_ref, slice(0, rest), partial(m_sc[0, :, :rest], acc_sc[0, :, :rest]))


def next_kernel(
    flag_ref, place_ref, q0_ref, q1_ref, k_ref, v_ref, o1_last, o0_last, o0_rest, o1,
    q_sc, m_sc, acc_sc, s0, s1, units,
):
    for slot, ref in ((0, q0_ref), (1, q1_ref)):
        q_sc[slot] = ref[...].reshape(BLOCK, HD)
    clear(m_sc, acc_sc)
    refs = (flag_ref, q_sc, k_ref, v_ref, m_sc, acc_sc, s0, s1)
    run_units(units, (0, 1), *refs)(list_units(units, flag_ref, (1,), 2))
    run_units(units, (2,), *refs)(list_units(units, flag_ref, (0,), 2))
    last = BLOCK - LANES
    put(o1, slice(0, last), partial(m_sc[1, :, :last], acc_sc[1, :, :last]))
    o1[:, last:BLOCK] = o1_last[...]
    part = partial(m_sc[0, :, last:], acc_sc[0, :, last:])
    put(o0_last, slice(0, LANES), part)
    put(o1, slice(BLOCK, BLOCK + QUARTER), [piece[:, -QUARTER:] for piece in part])

    @pl.when(place_ref[0] >= 2)
    def _():
        attend_rest(o0_rest, units, *refs)

    @pl.when(place_ref[0] < 2)
    def _():
        o0_rest[...] = jnp.zeros(o0_rest.shape, bf16)


def own_kernel(
    flag_ref, place_ref, q_ref, k_ref, v_ref, rest_ref, o_ref, q_sc, m_sc, acc_sc, s0, s1, units
):
    @pl.when(place_ref[0] >= 2)
    def _():
        o_ref[...] = rest_ref[...]

    @pl.when(place_ref[0] < 2)
    def _():
        q_sc[0] = q_ref[...].reshape(BLOCK, HD)
        clear(m_sc, acc_sc)
        attend_rest(o_ref, units, flag_ref, q_sc, k_ref, v_ref, m_sc, acc_sc, s0, s1)


def scratch(slots):
    vmem = pltpu.VMEM
    return [
        vmem((slots, BLOCK, HD), bf16),
        vmem((slots + 1, 8, BLOCK), f32),
        vmem((slots + 1, HD + STAT, BLOCK), f32),
        vmem((BLOCK, BLOCK), f32),
        vmem((BLOCK, BLOCK), f32),
        pltpu.SMEM((2, 16), jnp.int32),
    ]


def cost(units):
    return pl.CostEstimate(
        flops=4 * units * BLOCK * BLOCK * HD,
        bytes_accessed=8 << 20,
        transcendentals=units * BLOCK * BLOCK,
    )


def result(columns):
    return jax.ShapeDtypeStruct((HD + SENT, columns), bf16)


def attend_far(counts, flags, kv, q1, q2, q3):
    return pl.pallas_call(
        far_kernel,
        out_shape=[
            result(LANES),
            result(BLOCK + QUARTER),
            result(BLOCK + QUARTER),
            jax.ShapeDtypeStruct((4, BLOCK, HD), bf16),
            jax.ShapeDtypeStruct((4, HD + STAT, BLOCK), bf16),
        ],
        in_specs=[SM] * 2 + [VM] * 4,
        out_specs=[VM] * 5,
        scratch_shapes=scratch(4),
        compiler_params=PARAMS,
        cost_estimate=cost(10),
    )(counts, flags, kv, q1, q2, q3)


def attend_next(flags, place, q0, q1, k, v, last):
    return pl.pallas_call(
        next_kernel,
        out_shape=[result(LANES), result(BLOCK - LANES), result(BLOCK + QUARTER)],
        in_specs=[SM] * 2 + [VM] * 5,
        out_specs=[VM] * 3,
        scratch_shapes=scratch(2),
        compiler_params=PARAMS,
        cost_estimate=cost(4),
    )(flags, place, q0, q1, k, v, last)


def attend_own(flags, place, q, k, v, rest):
    return pl.pallas_call(
        own_kernel,
        out_shape=result(BLOCK - LANES),
        in_specs=[SM] * 2 + [VM] * 4,
        out_specs=VM,
        scratch_shapes=scratch(1),
        compiler_params=PARAMS,
        cost_estimate=cost(4),
    )(flags, place, q, k, v, rest)


def blend(stats, heads):
    levels = [stat[0:1] + stat[1:2] + stat[2:3] for stat in stats]
    top = levels[0]
    for level in levels[1:]:
        top = jnp.maximum(top, level)
    shares = [jnp.exp2(level - top) for level in levels]
    whole = sum(shares[1:], shares[0])
    total = sum(head.astype(f32) * (share / whole) for head, share in zip(heads, shares))
    return total.astype(bf16).T


def merge_kernel(x_ref, r0, r0_last, r1, r2, r3, o_ref):
    own = jnp.concatenate([r0[...], r0_last[...]], axis=1)
    stats, heads = [own[HD:].astype(f32)], [own[:HD]]
    for k, ref in ((1, r1), (2, r2), (3, r3)):
        stat = ref[HD:].astype(f32)
        row = lax.broadcasted_iota(jnp.int32, stat.shape, 0)
        stats.append(jnp.where(x_ref[0] >= k, stat, jnp.where(row == 0, LOW, 0.0)))
        heads.append(ref[:HD])
    own = blend([stat[:, :BLOCK] for stat in stats], [head[:, :BLOCK] for head in heads])
    tail = blend([stat[:, BLOCK:] for stat in stats[1:]], [head[:, BLOCK:] for head in heads[1:]])
    own = own.reshape(HEADS, ROWS, HD)
    before = jnp.concatenate([tail.reshape(8, ROWS, HD), own[: HEADS - 8]])
    for target, place in PAIR_ORDER:
        o_ref[target : target + 2, 0] = own[place : place + 2]
        o_ref[target : target + 2, 1] = before[place : place + 2]


def merge(x, parts):
    return pl.pallas_call(
        merge_kernel,
        out_shape=jax.ShapeDtypeStruct((HEADS, 2, ROWS, HD), bf16),
        in_specs=[SM] + [VM] * 5,
        out_specs=VM,
        compiler_params=PARAMS,
    )(x, *parts)


def finish_kernel(
    level_ref, first_ref, r_ref, latent_ref, latent_before_ref, entering_ref, gate_ref,
    updated_ref, advanced_ref,
):
    def update(which, level, residual):
        squares = jnp.zeros((ROWS, HD), f32)
        for h in range(HEADS):
            wide = r_ref[h, which].astype(f32)
            squares = squares + wide * wide
        mean = jnp.sum(squares, axis=-1, keepdims=True) * (1.0 / (HEADS * HD))
        factor = 1.0 / jnp.sqrt(mean + 1e-06)
        index = lax.broadcasted_iota(jnp.int32, (gate_ref.shape[0], HD), 0)
        mine = index.astype(f32) == level
        for h in range(HEADS):
            span = slice(h * HD, (h + 1) * HD)
            gate = jnp.sum(jnp.where(mine, gate_ref[:, span], 0.0), axis=0, keepdims=True)
            wide = r_ref[h, which].astype(f32)
            yield span, residual[0, :, span].astype(f32) + gate * (wide * factor)

    for span, value in update(0, level_ref[0].astype(f32), latent_ref):
        updated_ref[0, :, span] = value.astype(bf16)
    first = first_ref[0] == 1
    before = latent_before_ref[0, :1, HEADS * HD :].astype(f32)
    for span, value in update(1, before, latent_before_ref):
        advanced_ref[0, :, span] = jnp.where(first, entering_ref[:, span], value.astype(bf16))


def finish(level, first, returned, latent, latent_before, entering, gate_table):
    return pl.pallas_call(
        finish_kernel,
        out_shape=[jax.ShapeDtypeStruct(latent.shape, bf16)] * 2,
        in_specs=[SM] * 2 + [VM] * 5,
        out_specs=[VM] * 2,
        compiler_params=PARAMS,
    )(level, first, returned, latent, latent_before, entering, gate_table)


def local(
    queries, keys, values, latent, entering, noise_level, token_counts, block_mask, gate_table
):
    x = lax.axis_index("x")
    sources = [
        pltpu.with_memory_space_constraint(source, pltpu.HBM)
        for source in (queries, keys, values, latent)
    ]
    packed, latent_level = pack(noise_level, *sources)
    packed = lax.all_to_all(packed, HEAD_AXES, split_axis=0, concat_axis=0, tiled=True)
    packed, latent_level = lax.optimization_barrier((packed, latent_level))
    q, kv = unpack(packed)
    q1, q2, q3 = (
        lax.ppermute(q, "x", [(source, source - steps) for source in range(steps, 4)])
        for steps in (1, 2, 3)
    )
    kv = lax.all_to_all(kv, "y", split_axis=0, concat_axis=0, tiled=True)
    kv = kv.reshape(4, 4, 8, 2, ROWS, HD)
    q1, latent_level = lax.optimization_barrier((q1, latent_level))
    onward = [(s, s + 1) for s in range(15)]
    latent_before = lax.ppermute(latent_level, ("x", "zh"), onward)
    padded = jnp.concatenate([block_mask, jnp.zeros_like(block_mask)], axis=0)
    flags = lax.dynamic_slice(padded, (4 * x, 4 * x), (16, 4))
    counts = lax.dynamic_slice(token_counts, (4 * x,), (4,))
    place = x.reshape(1)
    last, part2, part3, k, v = attend_far(counts, flags, kv, q1, q2, q3)

    def onward_in_x(part, steps):
        return lax.ppermute(part, "x", [(source, source + steps) for source in range(4 - steps)])

    received3, received2 = onward_in_x(part3, 3), onward_in_x(part2, 2)
    own_last, own_rest, part1 = attend_next(flags, place, q, q1, k, v, last)
    received1 = onward_in_x(part1, 1)
    q, received2, received3, latent_before = lax.optimization_barrier(
        (q, received2, received3, latent_before)
    )
    own = attend_own(flags, place, q, k, v, own_rest)
    attended = merge(place, [own, own_last, received1, received2, received3])
    returned = lax.all_to_all(attended, HEAD_AXES, split_axis=0, concat_axis=0, tiled=True)
    first = ((x == 0) & (lax.axis_index("zh") == 0)).astype(jnp.int32).reshape(1)
    return tuple(
        finish(
            noise_level, first, returned, latent, latent_before, entering, gate_table
        )
    )


def solution(mesh):
    fine = Mesh(mesh.devices.reshape(4, 4, 4, 4, 2), ("x", "zh", "zl", "y", "c"))
    section, seq = ("x", "zh"), ("zl", "y", "c")
    placed = (
        P(section, seq, None),
        P(section, seq, None),
        P(section, seq, None),
        P(section, seq, None),
        P(seq, None),
        P(section),
        P(),
        P(),
        P(),
    )
    return jax.shard_map(
        local,
        mesh=fine,
        in_specs=placed,
        out_specs=(P(section, seq, None), P(section, seq, None)),
        check_vma=False,
    )
```

```python
import math

import jax
import jax.numpy as jnp
from jax import lax
from jax.experimental import pallas as pl
from jax.experimental.pallas import tpu as pltpu
from jax.sharding import Mesh
from jax.sharding import PartitionSpec as P

HD = 128
HEADS = 32
ROWS = 24
QUARTER = 192
BLOCK = 768
STAT = 16
SENT = 8
LANES = 256
SCALE = math.log2(math.e) / math.sqrt(HD)
LOW = -1e30
f32 = jnp.float32
bf16 = jnp.bfloat16

VM = pl.BlockSpec(memory_space=pltpu.VMEM)
SM = pl.BlockSpec(memory_space=pltpu.SMEM)
PARAMS = pltpu.CompilerParams(vmem_limit_bytes=48 * 2**20)
HEAD_AXES = ("zl", "zh", "c")
PAIR_ORDER = [(2 * (4 * zl + zh), 2 * (4 * zh + zl)) for zh in range(4) for zl in range(4)]


def pack_kernel(level_ref, q_hbm, k_hbm, v_hbm, latent_hbm, o_ref, latent_ref, buf, sems):
    sources = (q_hbm, k_hbm, v_hbm, latent_hbm)
    copies = [pltpu.make_async_copy(ref, buf.at[i], sems.at[i]) for i, ref in enumerate(sources)]
    for copy in copies:
        copy.start()
    latent_ref[0, :, HEADS * HD :] = jnp.full((ROWS, HD), level_ref[0], jnp.int32).astype(
        f32
    ).astype(bf16)
    for i in range(3):
        copies[i].wait()
        for h in range(HEADS):
            o_ref[h, i] = buf[i, 0, :, h * HD : (h + 1) * HD]
    copies[3].wait()
    latent_ref[0, :, : HEADS * HD] = buf[3, 0]


def pack(level, queries, keys, values, latent):
    hbm = pl.BlockSpec(memory_space=pltpu.HBM)
    return pl.pallas_call(
        pack_kernel,
        out_shape=[
            jax.ShapeDtypeStruct((HEADS, 3, ROWS, HD), bf16),
            jax.ShapeDtypeStruct((1, ROWS, HEADS * HD + HD), bf16),
        ],
        in_specs=[SM] + [hbm] * 4,
        out_specs=[VM] * 2,
        scratch_shapes=[
            pltpu.VMEM((4, 1, ROWS, HEADS * HD), bf16),
            pltpu.SemaphoreType.DMA((4,)),
        ],
        compiler_params=PARAMS,
    )(level, queries, keys, values, latent)


def unpack_kernel(packed_ref, q_ref, kv_ref):
    for source, place in PAIR_ORDER:
        q_ref[place : place + 2] = packed_ref[source : source + 2, 0]
        kv = packed_ref[source : source + 2, 1:]
        for copy in range(4):
            kv_ref[copy, place : place + 2] = kv


def unpack(packed):
    return pl.pallas_call(
        unpack_kernel,
        out_shape=[
            jax.ShapeDtypeStruct((HEADS, ROWS, HD), bf16),
            jax.ShapeDtypeStruct((4, HEADS, 2, ROWS, HD), bf16),
        ],
        in_specs=[VM],
        out_specs=[VM] * 2,
        compiler_params=PARAMS,
    )(packed)


def token_of(shape, dim):
    i = lax.broadcasted_iota(jnp.int32, shape, dim)
    one, nil = jnp.int32(1), jnp.int32(0)
    part = sum(jnp.where(i >= e * QUARTER, one, nil) for e in (1, 2, 3))
    inner = i - part * QUARTER
    run = sum(jnp.where(inner >= e * 48, one, nil) for e in (1, 2, 3))
    return inner + run * (QUARTER - 48) + part * 48


def list_units(units, flag_ref, slots, dummy):
    def build(e, n):
        slot, t = slots[0] + e // 4, e % 4
        active = flag_ref[slot * 4, t]
        for g in range(1, 4):
            active = active | flag_ref[slot * 4 + g, t]

        @pl.when(active == 1)
        def _():
            units[0, n] = slot
            units[1, n] = t

        return n + active

    n = lax.fori_loop(0, 4 * len(slots), build, jnp.int32(0))
    for i in range(2):
        units[0, n + i] = dummy
        units[1, n + i] = 0
    return n


def run_units(units, steps, flag_ref, q_sc, k_ref, v_ref, m_sc, acc_sc, s0, s1):
    real = q_sc.shape[0]
    lane = lax.broadcasted_iota(jnp.int32, (8, LANES), 1)

    def score(i, j, s):
        span = slice(j * LANES, (j + 1) * LANES)
        slot = jnp.minimum(units[0, i], real - 1)
        s[:, span] = lax.dot_general(
            k_ref[units[1, i]], q_sc[slot, span], (((1,), (1,)), ((), ())), preferred_element_type=f32
        )

    def weigh(i, j, s_read, s_write):
        span = slice(j * LANES, (j + 1) * LANES)
        slot, t = units[0, i], units[1, i]
        first = jnp.minimum(slot, real - 1) * 4
        flag = jnp.full((8, LANES), flag_ref[first + (j * LANES) // QUARTER, t], jnp.int32)
        for g in range(1, 4):
            if j * LANES < g * QUARTER < (j + 1) * LANES:
                flag = jnp.where(lane + j * LANES >= g * QUARTER, flag_ref[first + g, t], flag)
        on = flag == 1
        old = m_sc[slot, :, span]
        top = jnp.max(s_read[:, span], axis=0, keepdims=True) * SCALE
        new = jnp.where(on, jnp.maximum(old, top), old)
        m_sc[slot, :, span] = new
        a = jnp.exp2(old - new)
        p = jnp.exp2(s_read[:, span] * SCALE - jnp.where(on, new, -LOW)[:1]).astype(bf16)
        score(i + 1, j, s_write)
        part = jnp.dot(v_ref[t], p, preferred_element_type=f32)
        acc_sc[slot, :, span] = acc_sc[slot, :, span] * a[:1] + part

    def pair(h, carry):
        for j in steps:
            weigh(2 * h, j, s0, s1)
        for j in steps:
            weigh(2 * h + 1, j, s1, s0)
        return carry

    def run(n):
        for j in steps:
            score(0, j, s0)
        lax.fori_loop(0, (n + 1) // 2, pair, 0)

    return run


def clear(m_sc, acc_sc):
    m_sc[...] = jnp.full(m_sc.shape, LOW, f32)
    acc_sc[...] = jnp.zeros(acc_sc.shape, f32)


def partial(m, acc):
    total = acc[HD : HD + 1]
    some = total > 0.0
    safe = jnp.where(some, total, 1.0)
    level = jnp.where(some, m[:1] + jnp.log2(safe), LOW)
    hi = level.astype(bf16)
    mid = (level - hi.astype(f32)).astype(bf16)
    lo = (level - hi.astype(f32) - mid.astype(f32)).astype(bf16)
    stat = jnp.concatenate([hi, mid, lo, jnp.zeros((SENT - 3, level.shape[1]), bf16)], axis=0)
    return (acc[:HD] * (1.0 / safe)).astype(bf16), stat


def put(ref, span, part):
    head, stat = part
    ref[:HD, span] = head
    ref[HD:, span] = stat


def far_kernel(
    count_ref, flag_ref, kv_ref, q1_ref, q2_ref, q3_ref, o1_last, o2, o3, k_ref, v_ref,
    q_sc, m_sc, acc_sc, s0, s1, units,
):
    for slot, ref in ((1, q1_ref), (2, q2_ref), (3, q3_ref)):
        q_sc[slot] = ref[...].reshape(BLOCK, HD)

    token = token_of((BLOCK, HD), 0)
    token_row = token_of((STAT, BLOCK), 1)
    for t in range(4):
        k = jnp.concatenate([kv_ref[y, t, :, 0].reshape(QUARTER, HD) for y in range(4)])
        v = jnp.concatenate([kv_ref[y, t, :, 1].reshape(QUARTER, HD) for y in range(4)])
        valid = token < count_ref[t]
        k_ref[t] = jnp.where(valid, k, jnp.broadcast_to(k[0:1], k.shape))
        v_ref[t, :HD] = jnp.where(valid, v, jnp.zeros_like(v)).T
        v_ref[t, HD:] = jnp.where(token_row < count_ref[t], 1.0, 0.0).astype(bf16)

    clear(m_sc, acc_sc)
    refs = (flag_ref, q_sc, k_ref, v_ref, m_sc, acc_sc, s0, s1)
    run_units(units, (0, 1, 2), *refs)(list_units(units, flag_ref, (2, 3), 4))
    run_units(units, (2,), *refs)(list_units(units, flag_ref, (1,), 4))

    last = BLOCK - LANES
    part = partial(m_sc[1, :, last:], acc_sc[1, :, last:])
    put(o1_last, slice(0, LANES), part)
    for slot, ref in ((2, o2), (3, o3)):
        put(ref, slice(BLOCK, BLOCK + QUARTER), [piece[:, -QUARTER:] for piece in part])
        part = partial(m_sc[slot], acc_sc[slot])
        put(ref, slice(0, BLOCK), part)


def attend_rest(out_ref, units, flag_ref, q_sc, k_ref, v_ref, m_sc, acc_sc, s0, s1):
    dummy = q_sc.shape[0]
    refs = (flag_ref, q_sc, k_ref, v_ref, m_sc, acc_sc, s0, s1)
    run_units(units, (0, 1), *refs)(list_units(units, flag_ref, (0,), dummy))
    rest = BLOCK - LANES
    put(out_ref, slice(0, rest), partial(m_sc[0, :, :rest], acc_sc[0, :, :rest]))


def next_kernel(
    flag_ref, place_ref, q0_ref, q1_ref, k_ref, v_ref, o1_last, o0_last, o0_rest, o1,
    q_sc, m_sc, acc_sc, s0, s1, units,
):
    for slot, ref in ((0, q0_ref), (1, q1_ref)):
        q_sc[slot] = ref[...].reshape(BLOCK, HD)
    clear(m_sc, acc_sc)
    refs = (flag_ref, q_sc, k_ref, v_ref, m_sc, acc_sc, s0, s1)
    run_units(units, (0, 1), *refs)(list_units(units, flag_ref, (1,), 2))
    run_units(units, (2,), *refs)(list_units(units, flag_ref, (0,), 2))
    last = BLOCK - LANES
    put(o1, slice(0, last), partial(m_sc[1, :, :last], acc_sc[1, :, :last]))
    o1[:, last:BLOCK] = o1_last[...]
    part = partial(m_sc[0, :, last:], acc_sc[0, :, last:])
    put(o0_last, slice(0, LANES), part)
    put(o1, slice(BLOCK, BLOCK + QUARTER), [piece[:, -QUARTER:] for piece in part])

    @pl.when(place_ref[0] >= 2)
    def _():
        attend_rest(o0_rest, units, *refs)

    @pl.when(place_ref[0] < 2)
    def _():
        o0_rest[...] = jnp.zeros(o0_rest.shape, bf16)


def own_kernel(
    flag_ref, place_ref, q_ref, k_ref, v_ref, rest_ref, o_ref, q_sc, m_sc, acc_sc, s0, s1, units
):
    @pl.when(place_ref[0] >= 2)
    def _():
        o_ref[...] = rest_ref[...]

    @pl.when(place_ref[0] < 2)
    def _():
        q_sc[0] = q_ref[...].reshape(BLOCK, HD)
        clear(m_sc, acc_sc)
        attend_rest(o_ref, units, flag_ref, q_sc, k_ref, v_ref, m_sc, acc_sc, s0, s1)


def scratch(slots):
    vmem = pltpu.VMEM
    return [
        vmem((slots, BLOCK, HD), bf16),
        vmem((slots + 1, 8, BLOCK), f32),
        vmem((slots + 1, HD + STAT, BLOCK), f32),
        vmem((BLOCK, BLOCK), f32),
        vmem((BLOCK, BLOCK), f32),
        pltpu.SMEM((2, 16), jnp.int32),
    ]


def cost(units):
    return pl.CostEstimate(
        flops=4 * units * BLOCK * BLOCK * HD,
        bytes_accessed=8 << 20,
        transcendentals=units * BLOCK * BLOCK,
    )


def result(columns):
    return jax.ShapeDtypeStruct((HD + SENT, columns), bf16)


def attend_far(counts, flags, kv, q1, q2, q3):
    return pl.pallas_call(
        far_kernel,
        out_shape=[
            result(LANES),
            result(BLOCK + QUARTER),
            result(BLOCK + QUARTER),
            jax.ShapeDtypeStruct((4, BLOCK, HD), bf16),
            jax.ShapeDtypeStruct((4, HD + STAT, BLOCK), bf16),
        ],
        in_specs=[SM] * 2 + [VM] * 4,
        out_specs=[VM] * 5,
        scratch_shapes=scratch(4),
        compiler_params=PARAMS,
        cost_estimate=cost(10),
    )(counts, flags, kv, q1, q2, q3)


def attend_next(flags, place, q0, q1, k, v, last):
    return pl.pallas_call(
        next_kernel,
        out_shape=[result(LANES), result(BLOCK - LANES), result(BLOCK + QUARTER)],
        in_specs=[SM] * 2 + [VM] * 5,
        out_specs=[VM] * 3,
        scratch_shapes=scratch(2),
        compiler_params=PARAMS,
        cost_estimate=cost(4),
    )(flags, place, q0, q1, k, v, last)


def attend_own(flags, place, q, k, v, rest):
    return pl.pallas_call(
        own_kernel,
        out_shape=result(BLOCK - LANES),
        in_specs=[SM] * 2 + [VM] * 4,
        out_specs=VM,
        scratch_shapes=scratch(1),
        compiler_params=PARAMS,
        cost_estimate=cost(4),
    )(flags, place, q, k, v, rest)


def blend(stats, heads):
    levels = [stat[0:1] + stat[1:2] + stat[2:3] for stat in stats]
    top = levels[0]
    for level in levels[1:]:
        top = jnp.maximum(top, level)
    shares = [jnp.exp2(level - top) for level in levels]
    whole = sum(shares[1:], shares[0])
    total = sum(head.astype(f32) * (share / whole) for head, share in zip(heads, shares))
    return total.astype(bf16).T


def merge_kernel(x_ref, r0, r0_last, r1, r2, r3, o_ref):
    own = jnp.concatenate([r0[...], r0_last[...]], axis=1)
    stats, heads = [own[HD:].astype(f32)], [own[:HD]]
    for k, ref in ((1, r1), (2, r2), (3, r3)):
        stat = ref[HD:].astype(f32)
        row = lax.broadcasted_iota(jnp.int32, stat.shape, 0)
        stats.append(jnp.where(x_ref[0] >= k, stat, jnp.where(row == 0, LOW, 0.0)))
        heads.append(ref[:HD])
    own = blend([stat[:, :BLOCK] for stat in stats], [head[:, :BLOCK] for head in heads])
    tail = blend([stat[:, BLOCK:] for stat in stats[1:]], [head[:, BLOCK:] for head in heads[1:]])
    own = own.reshape(HEADS, ROWS, HD)
    before = jnp.concatenate([tail.reshape(8, ROWS, HD), own[: HEADS - 8]])
    for target, place in PAIR_ORDER:
        o_ref[target : target + 2, 0] = own[place : place + 2]
        o_ref[target : target + 2, 1] = before[place : place + 2]


def merge(x, parts):
    return pl.pallas_call(
        merge_kernel,
        out_shape=jax.ShapeDtypeStruct((HEADS, 2, ROWS, HD), bf16),
        in_specs=[SM] + [VM] * 5,
        out_specs=VM,
        compiler_params=PARAMS,
    )(x, *parts)


def finish_kernel(
    level_ref, first_ref, r_ref, latent_ref, latent_before_ref, entering_ref, gate_ref,
    updated_ref, advanced_ref,
):
    def update(which, level, residual):
        squares = jnp.zeros((ROWS, HD), f32)
        for h in range(HEADS):
            wide = r_ref[h, which].astype(f32)
            squares = squares + wide * wide
        mean = jnp.sum(squares, axis=-1, keepdims=True) * (1.0 / (HEADS * HD))
        factor = 1.0 / jnp.sqrt(mean + 1e-06)
        index = lax.broadcasted_iota(jnp.int32, (gate_ref.shape[0], HD), 0)
        mine = index.astype(f32) == level
        for h in range(HEADS):
            span = slice(h * HD, (h + 1) * HD)
            gate = jnp.sum(jnp.where(mine, gate_ref[:, span], 0.0), axis=0, keepdims=True)
            wide = r_ref[h, which].astype(f32)
            yield span, residual[0, :, span].astype(f32) + gate * (wide * factor)

    for span, value in update(0, level_ref[0].astype(f32), latent_ref):
        updated_ref[0, :, span] = value.astype(bf16)
    first = first_ref[0] == 1
    before = latent_before_ref[0, :1, HEADS * HD :].astype(f32)
    for span, value in update(1, before, latent_before_ref):
        advanced_ref[0, :, span] = jnp.where(first, entering_ref[:, span], value.astype(bf16))


def finish(level, first, returned, latent, latent_before, entering, gate_table):
    return pl.pallas_call(
        finish_kernel,
        out_shape=[jax.ShapeDtypeStruct(latent.shape, bf16)] * 2,
        in_specs=[SM] * 2 + [VM] * 5,
        out_specs=[VM] * 2,
        compiler_params=PARAMS,
    )(level, first, returned, latent, latent_before, entering, gate_table)


def local(
    queries, keys, values, latent, entering, noise_level, token_counts, block_mask, gate_table
):
    x = lax.axis_index("x")
    sources = [
        pltpu.with_memory_space_constraint(source, pltpu.HBM)
        for source in (queries, keys, values, latent)
    ]
    packed, latent_level = pack(noise_level, *sources)
    packed = lax.all_to_all(packed, HEAD_AXES, split_axis=0, concat_axis=0, tiled=True)
    packed, latent_level = lax.optimization_barrier((packed, latent_level))
    q, kv = unpack(packed)
    q1, q2, q3 = (
        lax.ppermute(q, "x", [(source, source - steps) for source in range(steps, 4)])
        for steps in (1, 2, 3)
    )
    kv = lax.all_to_all(kv, "y", split_axis=0, concat_axis=0, tiled=True)
    kv = kv.reshape(4, 4, 8, 2, ROWS, HD)
    q1, latent_level = lax.optimization_barrier((q1, latent_level))
    onward = [(s, s + 1) for s in range(15)]
    latent_before = lax.ppermute(latent_level, ("x", "zh"), onward)
    padded = jnp.concatenate([block_mask, jnp.zeros_like(block_mask)], axis=0)
    flags = lax.dynamic_slice(padded, (4 * x, 4 * x), (16, 4))
    counts = lax.dynamic_slice(token_counts, (4 * x,), (4,))
    place = x.reshape(1)
    last, part2, part3, k, v = attend_far(counts, flags, kv, q1, q2, q3)

    def onward_in_x(part, steps):
        return lax.ppermute(part, "x", [(source, source + steps) for source in range(4 - steps)])

    received3, received2 = onward_in_x(part3, 3), onward_in_x(part2, 2)
    own_last, own_rest, part1 = attend_next(flags, place, q, q1, k, v, last)
    received1 = onward_in_x(part1, 1)
    q, received2, latent_before = lax.optimization_barrier(
        (q, received2, latent_before)
    )
    own = attend_own(flags, place, q, k, v, own_rest)
    attended = merge(place, [own, own_last, received1, received2, received3])
    returned = lax.all_to_all(attended, HEAD_AXES, split_axis=0, concat_axis=0, tiled=True)
    first = ((x == 0) & (lax.axis_index("zh") == 0)).astype(jnp.int32).reshape(1)
    return tuple(
        finish(
            noise_level, first, returned, latent, latent_before, entering, gate_table
        )
    )


def solution(mesh):
    fine = Mesh(mesh.devices.reshape(4, 4, 4, 4, 2), ("x", "zh", "zl", "y", "c"))
    section, seq = ("x", "zh"), ("zl", "y", "c")
    placed = (
        P(section, seq, None),
        P(section, seq, None),
        P(section, seq, None),
        P(section, seq, None),
        P(seq, None),
        P(section),
        P(),
        P(),
        P(),
    )
    return jax.shard_map(
        local,
        mesh=fine,
        in_specs=placed,
        out_specs=(P(section, seq, None), P(section, seq, None)),
        check_vma=False,
    )
```
